256 devices in a mesh: rep: 4 (over y), fsdp: 64 (over z, x, core).
Axes of the slice: x: 4, y: 4, z: 8, core: 2. Of those that a mesh axis runs over, the one named last changes fastest.
Arguments:
- grads: bfloat16 [4, 256, 512, 512], P('rep', None, 'fsdp'), may hold values from -180 to 180
- left_factors: float32 [4, 64, 2, 512, 512], P('rep', 'fsdp'), may hold values from -1 to 1024, as said below
- right_factors: float32 [4, 64, 2, 512, 512], P('rep', 'fsdp'), may hold values from -1 to 1024, as said below
- owners: int32 [4, 64, 1], replicated, may hold values from 0 to 63; in each aligned block of 64 rows (0 to 63, 64 to 127, ..., all dimensions but the last counted through in order) at most 2 rows name the same one
Outputs:
- update: bfloat16 [256, 512, 512], P(None, 'fsdp')
- new_left: float32 [4, 64, 2, 512, 512], P('rep', 'fsdp')
- new_right: float32 [4, 64, 2, 512, 512], P('rep', 'fsdp')
The draws below stay inside these ranges and needn't reach their ends.
Inputs may be any that keep to these rules, and one draw needn't show every extreme that they name: `left_factors`: symmetric positive definite. `right_factors`: symmetric positive definite. `owners`: in each replica row at most 2 blocks share an owner, and in every draw some owner of some row has exactly 2.
All inputs are finite; a program needn't handle non-finite values.
Results may differ from the reference program's by a relative error of at most 0.018.
Values may be sent and summed in bfloat16 or wider, within the bound.
No kernel may reach another device: no remote copies, remote signals or barrier semaphores. Data moves between devices by JAX's collectives and lax.ppermute only.
A program may use at most 64 MiB of HBM per device.

```python
import math
import jax
import jax.numpy as jnp
import numpy as np
from jax import lax

BLK = 512
ITERS = 3
CAP = 2
NRB = 64
NB = 256
N_REP = 4
N_FSDP = 64


def spd_from(key, diagonal):
    lower = 0.5 * BLK
    shape = (N_REP, N_FSDP, CAP, BLK, BLK)
    noise = jax.random.uniform(key, shape, jnp.float32, -1.0, 1.0)
    symmetric = 0.5 * (noise + jnp.swapaxes(noise, -1, -2))
    identity = jnp.eye(BLK, dtype=jnp.float32)
    return symmetric * (lower / BLK) * (1.0 - identity) + identity * diagonal[..., :, None]


def heavy_scale(key, shape, largest):
    uniform_draw = jax.random.uniform(key, shape, jnp.float32, 0.0, 1.0)
    floored = jnp.maximum(uniform_draw, 1.0 / BLK) * BLK
    return largest / jnp.sqrt(floored)


def draw_grads(key, part):
    key = jax.random.fold_in(key, 11)
    first, second, third = jax.random.split(key, 3)
    shape = (N_REP, NB, BLK, BLK)
    base = jnp.clip(jax.random.normal(first, shape, jnp.float32), -3.5, 3.5)
    row_scale = heavy_scale(second, (1, NB, BLK, 1), 12.0)
    col_scale = heavy_scale(third, (1, NB, 1, BLK), 4.0)
    return (base * row_scale * col_scale).astype(jnp.bfloat16)


def draw_left_factors(key, part):
    key = jax.random.fold_in(key, 23)
    first, second = jax.random.split(key)
    lower = 0.5 * BLK
    shape = (N_REP, N_FSDP, CAP, BLK)
    diagonal = jnp.exp(jax.random.uniform(second, shape, jnp.float32, math.log(lower), math.log(3.0 * lower)))
    return spd_from(first, diagonal)


def draw_right_factors(key, part):
    key = jax.random.fold_in(key, 37)
    first, second = jax.random.split(key)
    lower = 0.5 * BLK
    shape = (N_REP, N_FSDP, CAP, BLK)
    diagonal = jnp.exp(jax.random.uniform(second, shape, jnp.float32, math.log(lower), math.log(3.0 * lower)))
    return spd_from(first, diagonal)


def deal_out(own_key, own, number, rows, count, top, limit, slope):
    sequence = jax.random.permutation(own_key, count)
    crowded, ordinary = portions_of(count, rows * top, limit, slope, True), portions_of(count, rows * top, limit, slope, False)
    places = jnp.arange(count)

    def named(sizes, turn):
        used = int((sizes > 0).sum())
        fixed = max(1, used // 4)
        passed = fixed + (places - fixed + turn * (used - fixed)) % max(1, count - fixed)
        return jnp.zeros((count,), jnp.int32).at[sequence[jnp.where(places < fixed, places, passed)]].set(jnp.asarray(sizes, jnp.int32))

    sizes = jnp.where(number % 4 == 0, named(crowded, number // 4), named(ordinary, number - number // 4 - 1))
    mixed = jax.random.permutation(jax.random.fold_in(own, 3), count)
    source_of, sink = mixed[0:count // 2 * 2:2], mixed[1:count // 2 * 2:2]
    margin = jnp.minimum(sizes[source_of] - 1, limit - sizes[sink]) // 2
    margin = jnp.where((source_of == sequence[0]) | (sink == sequence[0]) | (sizes[sink] == 0), 0, jnp.maximum(margin, 0))
    passed = jax.random.randint(jax.random.fold_in(own, 4), (count // 2,), 0, 1 << 20) % (margin + 1)
    sizes = sizes.at[source_of].add(-passed).at[sink].add(passed)
    labels = jnp.searchsorted(jnp.cumsum(sizes), jnp.arange(rows * top), side="right").astype(jnp.int32)
    grid = labels.reshape(top, rows).T
    grid = grid[jax.random.permutation(jax.random.fold_in(own, 1), rows)]
    turn = jax.random.randint(jax.random.fold_in(own, 2), (rows, 1), 0, top)
    return jnp.take_along_axis(grid, (jnp.arange(top)[None, :] + turn) % top, axis=1)


def portions_of(count, total, most, skew, full):
    portions = [(1 << 20) // math.isqrt(grade ** skew) + 1 for grade in range(1, count + 1)]
    largest = most if full else min(most, max(-(-total // count), total * portions[0] // sum(portions)))
    least = 1 if total - largest >= count - 1 else 0
    given, rest = [largest] + [least] * (count - 1), total - largest - least * (count - 1)
    while rest > 0:
        candidates = [i for i in range(1, count) if given[i] < largest] or [i for i in range(1, count) if given[i] < most]
        mass, budget = sum([portions[i] for i in candidates]), rest
        for i in candidates:
            extra = min(most - given[i], max(1, budget * portions[i] // mass), rest)
            given[i] = given[i] + extra
            rest = rest - extra
    return np.array(given)


def setup_inputs(seed: int = 0) -> dict:
    arg_keys = jax.random.split(jax.random.key(seed), 5)
    grads = draw_grads(jax.random.fold_in(arg_keys[4], 71), 0)
    left_factors = draw_left_factors(jax.random.fold_in(arg_keys[4], 71), 0)
    right_factors = draw_right_factors(jax.random.fold_in(arg_keys[4], 71), 0)
    owners_keys = jax.random.split(jax.random.fold_in(arg_keys[3], 1), N_REP * NRB // NRB)
    owners_turns = jax.random.permutation(jax.random.fold_in(arg_keys[3], 3), N_REP * NRB // NRB)
    owners = jax.vmap(lambda own, number: deal_out(jax.random.fold_in(arg_keys[3], 2), own, number, NRB, N_FSDP, 1, CAP, 2))(owners_keys, owners_turns).reshape((N_REP, NRB, 1))
    return {"grads": grads, "left_factors": left_factors, "right_factors": right_factors, "owners": owners}


def inverse_root(matrix):
    highest = lax.Precision.HIGHEST
    identity = jnp.eye(matrix.shape[-1], dtype=jnp.float32)
    frobenius = jnp.sqrt(lax.optimization_barrier(jnp.sum(matrix * matrix, axis=(1, 2))) + 1e-06)
    scaled_iterate = matrix / frobenius[:, None, None]
    root_iterate = identity[None]
    for sweep in range(ITERS):
        if sweep == 0:
            correction = 1.5 * identity - 0.5 * scaled_iterate
        else:
            product = jnp.einsum('sij,sjk->sik', root_iterate, scaled_iterate, precision=highest)
            correction = 1.5 * identity - 0.5 * product
        if sweep < ITERS - 1:
            scaled_iterate = jnp.einsum('sij,sjk->sik', scaled_iterate, correction, precision=highest)
        if sweep == 0:
            root_iterate = correction
        else:
            root_iterate = jnp.einsum('sij,sjk->sik', correction, root_iterate, precision=highest)
    return root_iterate

def owner_step(slot_grad, left_slots, right_slots):
    highest = lax.Precision.HIGHEST
    grad_wide = slot_grad.astype(jnp.float32)
    new_left = 0.9 * left_slots + 0.1 * jnp.einsum('sik,sjk->sij', grad_wide, grad_wide, precision=highest)
    new_right = 0.9 * right_slots + 0.1 * jnp.einsum('ski,skj->sij', grad_wide, grad_wide, precision=highest)
    root_left = inverse_root(new_left).astype(jnp.bfloat16)
    root_right = inverse_root(new_right).astype(jnp.bfloat16)
    half = jnp.einsum('sij,sjk->sik', root_left.astype(jnp.float32), grad_wide, precision=highest).astype(jnp.bfloat16)
    raw = jnp.einsum('sij,sjk->sik', half.astype(jnp.float32), root_right.astype(jnp.float32), precision=highest)
    grad_norm = lax.optimization_barrier(jnp.sum(grad_wide * grad_wide, axis=(1, 2)))
    raw_norm = lax.optimization_barrier(jnp.sum(raw * raw, axis=(1, 2)))
    factor = jnp.sqrt(grad_norm) * lax.rsqrt(raw_norm + 1e-06)
    slot_update = (raw * factor[:, None, None]).astype(jnp.bfloat16)
    return (new_left, new_right, slot_update)

def reference(grads, left_factors, right_factors, owners):
    gradient = lax.optimization_barrier(jnp.sum(grads.astype(jnp.float32), axis=0)).astype(jnp.bfloat16)
    gradient = gradient.reshape(N_REP, NRB, BLK, BLK)
    owner_ids = owners[:, :, 0]
    position = jnp.arange(NRB, dtype=jnp.int32)
    same_owner = owner_ids[:, :, None] == owner_ids[:, None, :]
    earlier = position[None, :] < position[:, None]
    slot_rank = lax.optimization_barrier(jnp.sum((same_owner & earlier[None]).astype(jnp.int32), axis=2))
    routing = (owner_ids[:, :, None, None] == jnp.arange(N_FSDP, dtype=jnp.int32)[:, None]) & (slot_rank[:, :, None, None] == jnp.arange(CAP, dtype=jnp.int32))
    routing_int = routing.astype(jnp.int32)
    block_of = lax.optimization_barrier(jnp.sum(routing_int * position[None, :, None, None], axis=1)).astype(jnp.int32)
    filled = lax.optimization_barrier(jnp.sum(routing_int, axis=1))
    row_index = jnp.arange(N_REP, dtype=jnp.int32)[:, None, None]
    picked = gradient[row_index, block_of]
    slot_grad = jnp.where(filled[:, :, :, None, None] > 0, picked, jnp.zeros_like(picked))

    def per_owner(items):
        return owner_step(items[0], items[1], items[2])
    new_left, new_right, slot_update = lax.map(per_owner, (slot_grad.reshape(N_REP * N_FSDP, CAP, BLK, BLK), left_factors.reshape(N_REP * N_FSDP, CAP, BLK, BLK), right_factors.reshape(N_REP * N_FSDP, CAP, BLK, BLK)))
    slot_update = slot_update.reshape(N_REP, N_FSDP, CAP, BLK, BLK)
    update = slot_update[jnp.arange(N_REP, dtype=jnp.int32)[:, None], owner_ids, slot_rank]
    update = update.reshape(NB, BLK, BLK)
    return (update, new_left.reshape(N_REP, N_FSDP, CAP, BLK, BLK), new_right.reshape(N_REP, N_FSDP, CAP, BLK, BLK))
```

```python
import functools

import jax
import jax.numpy as jnp
from jax import lax
from jax.experimental import pallas as pl
from jax.experimental.pallas import tpu as pltpu
from jax.sharding import PartitionSpec as P

BF16 = jnp.bfloat16
F32 = jnp.float32
VMEM_BYTES = 50 * 1024 * 1024


def routing_tables(owner_ids, fsdp_count, capacity):
    count = owner_ids.shape[0]
    position = jnp.arange(count, dtype=jnp.int32)
    same_owner = owner_ids[:, None] == owner_ids[None, :]
    earlier = position[None, :] < position[:, None]
    slot_rank = jnp.sum((same_owner & earlier).astype(jnp.int32), axis=1)
    slot_of = owner_ids * capacity + slot_rank
    slots = jnp.arange(fsdp_count * capacity, dtype=jnp.int32)
    holds = slot_of[None, :] == slots[:, None]
    block_of = count + jnp.sum(jnp.where(holds, position[None, :] - count, 0), axis=1)
    return block_of.astype(jnp.int32), slot_of.astype(jnp.int32)


def pack_kernel(table, own, first_a, first_b, second_a, second_b, out, held):
    half = first_a.shape[1]
    count = 2 * half
    for k, (first, second) in enumerate(((first_a, second_a), (first_b, second_b))):
        total = own[0, k].astype(F32) + first[0].astype(F32) + second[...].astype(F32)
        held[k * half : (k + 1) * half] = total
    held[count] = jnp.zeros(held.shape[1:], F32)
    owners, capacity = out.shape[0], out.shape[1]

    def move(o, carry):
        for s in range(capacity):
            out[o, s] = held[table[1 + o * capacity + s]].astype(BF16)
        return carry

    lax.fori_loop(0, owners, move, 0, unroll=4)


def dot(a, b, ca=1, cb=0):
    return lax.dot_general(a, b, (((ca,), (cb,)), ((), ())), preferred_element_type=F32)


def inverse_root(matrix, identity):
    y = matrix * lax.rsqrt(jnp.sum(matrix * matrix) + 1e-06)
    yb = y.astype(BF16)
    y2 = dot(yb, yb)
    s = 2.25 * y - 1.5 * y2 + 0.25 * dot(y2.astype(BF16), yb)
    sb = s.astype(BF16)
    s2 = dot(sb, sb)
    q = -2.4375 * s + 1.6875 * s2 + dot(s2.astype(BF16), (0.0625 * s2 - 0.5625 * s).astype(BF16))
    z = 3.375 * identity + 1.5 * q - 1.125 * y - 0.5 * dot(yb, q.astype(BF16))
    return z.astype(BF16)


def owner_kernel(arrived, left, right, new_left, new_right, out):
    n = left.shape[1]
    wide = arrived[:, 0].astype(F32).reshape(n, n)
    grad_norm = jnp.sum(wide * wide)
    grad = wide.astype(BF16)
    row = lax.broadcasted_iota(jnp.int32, (n, n), 0)
    col = lax.broadcasted_iota(jnp.int32, (n, n), 1)
    identity = (row == col).astype(F32)
    nl = 0.9 * left[0] + 0.1 * dot(grad, grad, 1, 1)
    nr = 0.9 * right[0] + 0.1 * dot(grad, grad, 0, 0)
    new_left[0] = nl
    new_right[0] = nr
    root_left = inverse_root(nl, identity)
    root_right = inverse_root(nr, identity)
    half = dot(root_left, grad).astype(BF16)
    raw = dot(half, root_right)
    raw_norm = jnp.sum(raw * raw)
    factor = jnp.sqrt(grad_norm) * lax.rsqrt(raw_norm + 1e-06)
    out[:, 0] = (raw * factor).reshape(out.shape[0], out.shape[2], out.shape[3]).astype(BF16)


def unpack_kernel(table, slots, out_a, out_b):
    half = out_a.shape[0]

    def move(j, carry):
        out_a[j] = slots[table[j]]
        out_b[j] = slots[table[half + j]]
        return carry

    lax.fori_loop(0, half, move, 0, unroll=4)


def place_kernel(table, *refs):
    parts, out, sems = refs[:8], refs[8], refs[9]
    copies = [
        pltpu.make_async_copy(part, out.at[table[i // 2], i % 2], sems.at[i]) for i, part in enumerate(parts)
    ]
    for copy in copies:
        copy.start()
    for copy in copies:
        copy.wait()


def shards(grads, left_factors, right_factors, owners):
    reps = lax.axis_size("rep")
    fsdp = lax.axis_size("fsdp")
    r = lax.axis_index("rep").astype(jnp.int32)
    rows, width = grads.shape[2], grads.shape[3]
    capacity, order = left_factors.shape[2], left_factors.shape[3]
    per_row = grads.shape[1] // reps
    half = per_row // 2
    own_owners = lax.dynamic_index_in_dim(owners[:, :, 0], r, 0, keepdims=False)
    block_of, slot_of = routing_tables(own_owners, fsdp, capacity)

    swap1 = [(i, i ^ 1) for i in range(reps)]
    swap3 = [(i, i ^ 3) for i in range(reps)]
    parts = grads.reshape(reps, 2, half, rows, width)

    def part(k, h):
        return lax.dynamic_index_in_dim(parts[:, h], r ^ k, 0, keepdims=False)

    first_a = lax.ppermute(jnp.stack([part(1, 0), part(2, 0)]), "rep", swap1)
    first_b = lax.ppermute(jnp.stack([part(3, 1), part(2, 1)]), "rep", swap3)
    second_a = lax.ppermute(part(3, 0) + first_a[1], "rep", swap3)
    second_b = lax.ppermute(part(1, 1) + first_b[1], "rep", swap1)

    outgoing = pl.pallas_call(
        pack_kernel,
        out_shape=jax.ShapeDtypeStruct((fsdp, capacity, rows, width), BF16),
        grid_spec=pltpu.PrefetchScalarGridSpec(
            num_scalar_prefetch=1,
            grid=(1,),
            in_specs=[
                pl.BlockSpec((1, 2, half, rows, width), lambda i, t: (t[0], 0, 0, 0, 0)),
                pl.BlockSpec((1, half, rows, width), lambda i, t: (0, 0, 0, 0)),
                pl.BlockSpec((1, half, rows, width), lambda i, t: (0, 0, 0, 0)),
                pl.BlockSpec((half, rows, width), lambda i, t: (0, 0, 0)),
                pl.BlockSpec((half, rows, width), lambda i, t: (0, 0, 0)),
            ],
            out_specs=pl.BlockSpec((fsdp, capacity, rows, width), lambda i, t: (0, 0, 0, 0)),
            scratch_shapes=[pltpu.VMEM((per_row + 1, rows, width), F32)],
        ),
        compiler_params=pltpu.CompilerParams(vmem_limit_bytes=VMEM_BYTES),
        name="pack",
    )(jnp.concatenate([r[None], block_of]), parts, first_a, first_b, second_a, second_b)

    arrived = lax.all_to_all(outgoing, "fsdp", split_axis=0, concat_axis=0, tiled=True)

    factor_spec = pl.BlockSpec((1, order, order), lambda s: (s, 0, 0))
    slot_spec = pl.BlockSpec((fsdp, 1, rows, width), lambda s: (0, s, 0, 0))
    new_left, new_right, slot_update = pl.pallas_call(
        owner_kernel,
        grid=(capacity,),
        in_specs=[slot_spec, factor_spec, factor_spec],
        out_specs=[factor_spec, factor_spec, slot_spec],
        out_shape=[
            jax.ShapeDtypeStruct((capacity, order, order), F32),
            jax.ShapeDtypeStruct((capacity, order, order), F32),
            jax.ShapeDtypeStruct((fsdp, capacity, rows, width), BF16),
        ],
        compiler_params=pltpu.CompilerParams(vmem_limit_bytes=VMEM_BYTES),
        name="owner",
    )(arrived, left_factors[0, 0], right_factors[0, 0])

    returned = lax.all_to_all(slot_update, "fsdp", split_axis=0, concat_axis=0, tiled=True)

    whole = pl.BlockSpec((half, rows, width), lambda i, t: (0, 0, 0))
    mine_a, mine_b = pl.pallas_call(
        unpack_kernel,
        out_shape=[jax.ShapeDtypeStruct((half, rows, width), BF16)] * 2,
        grid_spec=pltpu.PrefetchScalarGridSpec(
            num_scalar_prefetch=1,
            grid=(1,),
            in_specs=[pl.BlockSpec((fsdp * capacity, rows, width), lambda i, t: (0, 0, 0))],
            out_specs=[whole, whole],
        ),
        compiler_params=pltpu.CompilerParams(vmem_limit_bytes=VMEM_BYTES),
        name="unpack",
    )(slot_of, returned.reshape(fsdp * capacity, rows, width))

    plus = [(i, (i + 1) % reps) for i in range(reps)]
    minus = [(i, (i - 1) % reps) for i in range(reps)]
    left_a = lax.ppermute(mine_a, "rep", plus)
    right_b = lax.ppermute(mine_b, "rep", minus)
    left_b = lax.ppermute(mine_b, "rep", plus)
    right_a = lax.ppermute(mine_a, "rep", minus)
    far_a = lax.ppermute(left_a, "rep", plus)
    far_b = lax.ppermute(right_b, "rep", minus)
    places = jnp.stack([r, (r + 3) % reps, (r + 1) % reps, (r + 2) % reps])
    update = pl.pallas_call(
        place_kernel,
        out_shape=jax.ShapeDtypeStruct((reps, 2, half, rows, width), BF16),
        grid_spec=pltpu.PrefetchScalarGridSpec(
            num_scalar_prefetch=1,
            grid=(1,),
            in_specs=[pl.BlockSpec(memory_space=pl.ANY)] * 8,
            out_specs=pl.BlockSpec(memory_space=pl.ANY),
            scratch_shapes=[pltpu.SemaphoreType.DMA((8,))],
        ),
        name="place",
    )(places, mine_a, mine_b, left_a, left_b, right_a, right_b, far_a, far_b)
    return (update.reshape(reps * per_row, rows, width), new_left[None, None], new_right[None, None])


def solution(mesh):
    in_specs = (
        P("rep", None, "fsdp", None),
        P("rep", "fsdp", None, None, None),
        P("rep", "fsdp", None, None, None),
        P(),
    )
    out_specs = (
        P(None, "fsdp", None),
        P("rep", "fsdp", None, None, None),
        P("rep", "fsdp", None, None, None),
    )
    return jax.shard_map(shards, mesh=mesh, in_specs=in_specs, out_specs=out_specs, check_vma=False)
```

```python
import functools

import jax
import jax.numpy as jnp
from jax import lax
from jax.experimental import pallas as pl
from jax.experimental.pallas import tpu as pltpu
from jax.sharding import PartitionSpec as P

BF16 = jnp.bfloat16
F32 = jnp.float32
VMEM_BYTES = 36 * 1024 * 1024


def routing_tables(owner_ids, fsdp_count, capacity):
    count = owner_ids.shape[0]
    position = jnp.arange(count, dtype=jnp.int32)
    same_owner = owner_ids[:, None] == owner_ids[None, :]
    earlier = position[None, :] < position[:, None]
    slot_rank = jnp.sum((same_owner & earlier).astype(jnp.int32), axis=1)
    slot_of = owner_ids * capacity + slot_rank
    slots = jnp.arange(fsdp_count * capacity, dtype=jnp.int32)
    holds = slot_of[None, :] == slots[:, None]
    block_of = count + jnp.sum(jnp.where(holds, position[None, :] - count, 0), axis=1)
    return block_of.astype(jnp.int32), slot_of.astype(jnp.int32)


def pick_kernel(places, table, parts, *refs):
    outs, sems = refs[:-1], refs[-1]
    copies = []
    for i, (k, h, target, row) in enumerate(places):
        copies.append(pltpu.make_async_copy(parts.at[table[k], h], outs[target].at[row], sems.at[i]))
    for copy in copies:
        copy.start()
    for copy in copies:
        copy.wait()


def relay_kernel(kept, first, out):
    out[...] = (kept[0].astype(F32) + first[1].astype(F32)).astype(BF16)


def presum_kernel(own, first_a, first_b, out):
    half = first_a.shape[1]
    for k, first in enumerate((first_a, first_b)):
        out[k * half : (k + 1) * half] = own[k].astype(F32) + first[0].astype(F32)


def pack_kernel(table, presum, second_a, second_b, out, held):
    half = second_a.shape[0]
    count = 2 * half
    for k, second in enumerate((second_a, second_b)):
        rows = slice(k * half, (k + 1) * half)
        held[rows] = presum[rows] + second[...].astype(F32)
    held[count] = jnp.zeros(held.shape[1:], F32)
    owners, capacity = out.shape[0], out.shape[1]

    def move(o, carry):
        for s in range(capacity):
            out[o, s] = held[table[o * capacity + s]].astype(BF16)
        return carry

    lax.fori_loop(0, owners, move, 0, unroll=4)


def dot(a, b, ca=1, cb=0):
    return lax.dot_general(a, b, (((ca,), (cb,)), ((), ())), preferred_element_type=F32)


def inverse_roots(matrices, identity):
    ys = [m * lax.rsqrt(jnp.sum(m * m) + 1e-06) for m in matrices]
    ybs = [y.astype(BF16) for y in ys]
    y2s = [dot(b, b) for b in ybs]
    ss = [2.25 * y - 1.5 * y2 + 0.25 * dot(y2.astype(BF16), b) for y, y2, b in zip(ys, y2s, ybs)]
    sbs = [s.astype(BF16) for s in ss]
    s2s = [dot(s, s) for s in sbs]
    qs = [
        -2.4375 * s + 1.6875 * s2 + dot(s2.astype(BF16), (0.0625 * s2 - 0.5625 * s).astype(BF16))
        for s, s2 in zip(ss, s2s)
    ]
    zs = [
        3.375 * identity + 1.5 * q - 1.125 * y - 0.5 * dot(b, q.astype(BF16)) for q, y, b in zip(qs, ys, ybs)
    ]
    return [z.astype(BF16) for z in zs]


def owner_kernel(arrived, left, right, new_left, new_right, out, held_left, held_right, sems):
    capacity, n = left.shape[0], left.shape[1]
    row = lax.broadcasted_iota(jnp.int32, (n, n), 0)
    col = lax.broadcasted_iota(jnp.int32, (n, n), 1)
    identity = (row == col).astype(F32)
    copies, grads, norms, factors = [], [], [], []
    for s in range(capacity):
        wide = arrived[:, s].astype(F32).reshape(n, n)
        grad = wide.astype(BF16)
        turned = grad.T
        new = (
            0.9 * left[s] + 0.1 * dot(grad, grad, 1, 1),
            0.9 * right[s] + 0.1 * dot(turned, turned, 1, 1),
        )
        for k, (held, target) in enumerate(((held_left, new_left), (held_right, new_right))):
            held[s] = new[k]
            copies.append(pltpu.make_async_copy(held.at[s], target.at[s], sems.at[2 * s + k]))
            copies[-1].start()
        grads.append(grad)
        norms.append(jnp.sum(wide * wide))
        factors.append(new)
    for s in range(capacity):
        root_left, root_right = inverse_roots(factors[s], identity)
        half = dot(root_left, grads[s]).astype(BF16)
        raw = dot(half, root_right)
        factor = jnp.sqrt(norms[s]) * lax.rsqrt(jnp.sum(raw * raw) + 1e-06)
        out[:, s] = (raw * factor).reshape(out.shape[0], out.shape[2], out.shape[3]).astype(BF16)
    for copy in copies:
        copy.wait()


def unpack_kernel(table, slots, out_a, out_b):
    half = out_a.shape[0]

    def move(j, carry):
        out_a[j] = slots[table[j]]
        out_b[j] = slots[table[half + j]]
        return carry

    lax.fori_loop(0, half, move, 0, unroll=4)


def place_near_kernel(table, *refs):
    parts, out = refs[:6], refs[6]
    for k in range(3):

        @pl.when(pl.program_id(0) == k)
        def _():
            out[0, 0] = parts[2 * k][...]
            out[0, 1] = parts[2 * k + 1][...]


def place_far_kernel(table, far_a, far_b, near, out):
    out[0, 0] = far_a[...]
    out[0, 1] = far_b[...]


def shards(grads, left_factors, right_factors, owners):
    reps = lax.axis_size("rep")
    fsdp = lax.axis_size("fsdp")
    r = lax.axis_index("rep").astype(jnp.int32)
    rows, width = grads.shape[2], grads.shape[3]
    capacity, order = left_factors.shape[2], left_factors.shape[3]
    per_row = grads.shape[1] // reps
    half = per_row // 2
    own_owners = lax.dynamic_index_in_dim(owners[:, :, 0], r, 0, keepdims=False)
    block_of, slot_of = routing_tables(own_owners, fsdp, capacity)

    swap1 = [(i, i ^ 1) for i in range(reps)]
    swap3 = [(i, i ^ 3) for i in range(reps)]
    parts = grads.reshape(reps, 2, half, rows, width)
    params = pltpu.CompilerParams(vmem_limit_bytes=VMEM_BYTES)
    half_shape = jax.ShapeDtypeStruct((half, rows, width), BF16)
    half_spec = pl.BlockSpec((half, rows, width), lambda i, t: (0, 0, 0))

    in_vmem = pl.BlockSpec(memory_space=pltpu.VMEM)
    in_hbm = pl.BlockSpec(memory_space=pltpu.HBM)
    ranks = jnp.stack([r ^ k for k in range(4)])

    def pick(name, *groups):
        places = [(k, h, o, i) for o, group in enumerate(groups) for i, (k, h) in enumerate(group)]
        return pl.pallas_call(
            functools.partial(pick_kernel, places),
            out_shape=[jax.ShapeDtypeStruct((len(group), half, rows, width), BF16) for group in groups],
            grid_spec=pltpu.PrefetchScalarGridSpec(
                num_scalar_prefetch=1,
                grid=(1,),
                in_specs=[in_hbm],
                out_specs=[in_vmem] * len(groups),
                scratch_shapes=[pltpu.SemaphoreType.DMA((len(places),))],
            ),
            compiler_params=params,
            name=name,
        )(ranks, parts)

    (send_a,) = pick("pick_a", [(1, 0), (2, 0)])
    (send_b,) = pick("pick_b", [(3, 1), (2, 1)])
    first_a = lax.ppermute(send_a, "rep", swap1)
    first_b = lax.ppermute(send_b, "rep", swap3)
    kept_a, kept_b, own = pick("pick_kept", [(3, 0)], [(1, 1)], [(0, 0), (0, 1)])

    def relay(kept, first):
        return pl.pallas_call(
            relay_kernel,
            in_specs=[in_vmem] * 2,
            out_specs=in_vmem,
            out_shape=half_shape,
            compiler_params=params,
            name="relay",
        )(kept, first)

    second_a = lax.ppermute(relay(kept_a, first_a), "rep", swap3)
    second_b = lax.ppermute(relay(kept_b, first_b), "rep", swap1)
    presum = pl.pallas_call(
        presum_kernel,
        in_specs=[in_vmem] * 3,
        out_specs=in_vmem,
        out_shape=jax.ShapeDtypeStruct((per_row, rows, width), F32),
        compiler_params=params,
        name="presum",
    )(own, first_a, first_b)

    outgoing = pl.pallas_call(
        pack_kernel,
        out_shape=jax.ShapeDtypeStruct((fsdp, capacity, rows, width), BF16),
        grid_spec=pltpu.PrefetchScalarGridSpec(
            num_scalar_prefetch=1,
            grid=(1,),
            in_specs=[pl.BlockSpec((per_row, rows, width), lambda i, t: (0, 0, 0)), half_spec, half_spec],
            out_specs=pl.BlockSpec((fsdp, capacity, rows, width), lambda i, t: (0, 0, 0, 0)),
            scratch_shapes=[pltpu.VMEM((per_row + 1, rows, width), F32)],
        ),
        compiler_params=params,
        name="pack",
    )(block_of, presum, second_a, second_b)

    arrived = lax.all_to_all(outgoing, "fsdp", split_axis=0, concat_axis=0, tiled=True)

    anywhere = pl.BlockSpec(memory_space=pl.ANY)
    factors = jax.ShapeDtypeStruct((capacity, order, order), F32)
    new_left, new_right, slot_update = pl.pallas_call(
        owner_kernel,
        in_specs=[in_vmem, in_vmem, in_vmem],
        out_specs=[anywhere, anywhere, in_vmem],
        out_shape=[factors, factors, jax.ShapeDtypeStruct((fsdp, capacity, rows, width), BF16)],
        scratch_shapes=[
            pltpu.VMEM((capacity, order, order), F32),
            pltpu.VMEM((capacity, order, order), F32),
            pltpu.SemaphoreType.DMA((2 * capacity,)),
        ],
        compiler_params=params,
        name="owner",
    )(arrived, left_factors[0, 0], right_factors[0, 0])

    returned = lax.all_to_all(slot_update, "fsdp", split_axis=0, concat_axis=0, tiled=True)

    mine_a, mine_b = pl.pallas_call(
        unpack_kernel,
        out_shape=[half_shape] * 2,
        grid_spec=pltpu.PrefetchScalarGridSpec(
            num_scalar_prefetch=1,
            grid=(1,),
            in_specs=[pl.BlockSpec((fsdp * capacity, rows, width), lambda i, t: (0, 0, 0))],
            out_specs=[half_spec, half_spec],
        ),
        compiler_params=params,
        name="unpack",
    )(slot_of, returned.reshape(fsdp * capacity, rows, width))

    plus = [(i, (i + 1) % reps) for i in range(reps)]
    minus = [(i, (i - 1) % reps) for i in range(reps)]
    left_a = lax.ppermute(mine_a, "rep", plus)
    right_b = lax.ppermute(mine_b, "rep", minus)
    left_b = lax.ppermute(mine_b, "rep", plus)
    right_a = lax.ppermute(mine_a, "rep", minus)
    far_a = lax.ppermute(left_a, "rep", plus)
    far_b = lax.ppermute(right_b, "rep", minus)
    update_shape = jax.ShapeDtypeStruct((reps, 2, half, rows, width), BF16)
    row_spec = pl.BlockSpec((1, 2, half, rows, width), lambda i, t: (t[i], 0, 0, 0, 0))
    near = pl.pallas_call(
        place_near_kernel,
        out_shape=update_shape,
        grid_spec=pltpu.PrefetchScalarGridSpec(
            num_scalar_prefetch=1, grid=(3,), in_specs=[half_spec] * 6, out_specs=row_spec
        ),
        compiler_params=params,
        name="place_near",
    )(jnp.stack([r, (r + 3) % reps, (r + 1) % reps]), mine_a, mine_b, left_a, left_b, right_a, right_b)
    update = pl.pallas_call(
        place_far_kernel,
        out_shape=update_shape,
        grid_spec=pltpu.PrefetchScalarGridSpec(
            num_scalar_prefetch=1, grid=(1,), in_specs=[half_spec, half_spec, anywhere], out_specs=row_spec
        ),
        input_output_aliases={3: 0},
        compiler_params=params,
        name="place_far",
    )(((r + 2) % reps)[None], far_a, far_b, near)
    return (update.reshape(reps * per_row, rows, width), new_left[None, None], new_right[None, None])


def solution(mesh):
    in_specs = (
        P("rep", None, "fsdp", None),
        P("rep", "fsdp", None, None, None),
        P("rep", "fsdp", None, None, None),
        P(),
    )
    out_specs = (
        P(None, "fsdp", None),
        P("rep", "fsdp", None, None, None),
        P("rep", "fsdp", None, None, None),
    )
    return jax.shard_map(shards, mesh=mesh, in_specs=in_specs, out_specs=out_specs, check_vma=False)
```

```python
import functools

import jax
import jax.numpy as jnp
from jax import lax
from jax.experimental import pallas as pl
from jax.experimental.pallas import tpu as pltpu
from jax.sharding import PartitionSpec as P

BF16 = jnp.bfloat16
F32 = jnp.float32
VMEM_BYTES = 36 * 1024 * 1024


def routing_tables(owner_ids, fsdp_count, capacity):
    count = owner_ids.shape[0]
    position = jnp.arange(count, dtype=jnp.int32)
    same_owner = owner_ids[:, None] == owner_ids[None, :]
    earlier = position[None, :] < position[:, None]
    slot_rank = jnp.sum((same_owner & earlier).astype(jnp.int32), axis=1)
    slot_of = owner_ids * capacity + slot_rank
    slots = jnp.arange(fsdp_count * capacity, dtype=jnp.int32)
    holds = slot_of[None, :] == slots[:, None]
    block_of = count + jnp.sum(jnp.where(holds, position[None, :] - count, 0), axis=1)
    return block_of.astype(jnp.int32), slot_of.astype(jnp.int32)


def pick_kernel(places, table, parts, *refs):
    outs, sems = refs[:-1], refs[-1]
    copies = []
    for i, (k, h, target, row) in enumerate(places):
        copies.append(pltpu.make_async_copy(parts.at[table[k], h], outs[target].at[row], sems.at[i]))
    for copy in copies:
        copy.start()
    for copy in copies:
        copy.wait()


def relay_kernel(kept, relayed, out):
    out[...] = (kept[0].astype(F32) + relayed[...].astype(F32)).astype(BF16)


def presum_kernel(own, direct_a, direct_b, out):
    half = direct_a.shape[1]
    for k, direct in enumerate((direct_a, direct_b)):
        out[k * half : (k + 1) * half] = own[k].astype(F32) + direct[0].astype(F32)


def pack_kernel(table, presum, second_a, second_b, out, held):
    half = second_a.shape[0]
    count = 2 * half
    for k, second in enumerate((second_a, second_b)):
        rows = slice(k * half, (k + 1) * half)
        held[rows] = presum[rows] + second[...].astype(F32)
    held[count] = jnp.zeros(held.shape[1:], F32)
    owners, capacity = out.shape[0], out.shape[1]

    def move(o, carry):
        for s in range(capacity):
            out[o, s] = held[table[o * capacity + s]].astype(BF16)
        return carry

    lax.fori_loop(0, owners, move, 0, unroll=4)


def dot(a, b, ca=1, cb=0):
    return lax.dot_general(a, b, (((ca,), (cb,)), ((), ())), preferred_element_type=F32)


def inverse_roots(matrices, identity):
    ys = [m * lax.rsqrt(jnp.sum(m * m) + 1e-06) for m in matrices]
    ybs = [y.astype(BF16) for y in ys]
    y2s = [dot(b, b) for b in ybs]
    ss = [2.25 * y - 1.5 * y2 + 0.25 * dot(y2.astype(BF16), b) for y, y2, b in zip(ys, y2s, ybs)]
    sbs = [s.astype(BF16) for s in ss]
    s2s = [dot(s, s) for s in sbs]
    qs = [
        -2.4375 * s + 1.6875 * s2 + dot(s2.astype(BF16), (0.0625 * s2 - 0.5625 * s).astype(BF16))
        for s, s2 in zip(ss, s2s)
    ]
    zs = [
        3.375 * identity + 1.5 * q - 1.125 * y - 0.5 * dot(b, q.astype(BF16)) for q, y, b in zip(qs, ys, ybs)
    ]
    return [z.astype(BF16) for z in zs]


def owner_kernel(arrived, left, right, new_left, new_right, out, held_left, held_right, sems):
    capacity, n = left.shape[0], left.shape[1]
    row = lax.broadcasted_iota(jnp.int32, (n, n), 0)
    col = lax.broadcasted_iota(jnp.int32, (n, n), 1)
    identity = (row == col).astype(F32)
    copies, grads, norms, factors = [], [], [], []
    for s in range(capacity):
        wide = arrived[:, s].astype(F32).reshape(n, n)
        grad = wide.astype(BF16)
        turned = grad.T
        new = (
            0.9 * left[s] + 0.1 * dot(grad, grad, 1, 1),
            0.9 * right[s] + 0.1 * dot(turned, turned, 1, 1),
        )
        for k, (held, target) in enumerate(((held_left, new_left), (held_right, new_right))):
            held[s] = new[k]
            copies.append(pltpu.make_async_copy(held.at[s], target.at[s], sems.at[2 * s + k]))
            copies[-1].start()
        grads.append(grad)
        norms.append(jnp.sum(wide * wide))
        factors.append(new)
    for s in range(capacity):
        root_left, root_right = inverse_roots(factors[s], identity)
        half = dot(root_left, grads[s]).astype(BF16)
        raw = dot(half, root_right)
        factor = jnp.sqrt(norms[s]) * lax.rsqrt(jnp.sum(raw * raw) + 1e-06)
        out[:, s] = (raw * factor).reshape(out.shape[0], out.shape[2], out.shape[3]).astype(BF16)
    for copy in copies:
        copy.wait()


def unpack_kernel(table, slots, out_a, out_b):
    half = out_a.shape[0]

    def move(j, carry):
        out_a[j] = slots[table[j]]
        out_b[j] = slots[table[half + j]]
        return carry

    lax.fori_loop(0, half, move, 0, unroll=4)


def place_near_kernel(table, *refs):
    parts, out = refs[:6], refs[6]
    for k in range(3):

        @pl.when(pl.program_id(0) == k)
        def _():
            out[0, 0] = parts[2 * k][...]
            out[0, 1] = parts[2 * k + 1][...]


def place_far_kernel(table, far_a, far_b, near, out):
    out[0, 0] = far_a[...]
    out[0, 1] = far_b[...]


def shards(grads, left_factors, right_factors, owners):
    reps = lax.axis_size("rep")
    fsdp = lax.axis_size("fsdp")
    r = lax.axis_index("rep").astype(jnp.int32)
    rows, width = grads.shape[2], grads.shape[3]
    capacity, order = left_factors.shape[2], left_factors.shape[3]
    per_row = grads.shape[1] // reps
    half = per_row // 2
    own_owners = lax.dynamic_index_in_dim(owners[:, :, 0], r, 0, keepdims=False)
    block_of, slot_of = routing_tables(own_owners, fsdp, capacity)

    swap1 = [(i, i ^ 1) for i in range(reps)]
    swap3 = [(i, i ^ 3) for i in range(reps)]
    parts = grads.reshape(reps, 2, half, rows, width)
    params = pltpu.CompilerParams(vmem_limit_bytes=VMEM_BYTES)
    half_shape = jax.ShapeDtypeStruct((half, rows, width), BF16)
    half_spec = pl.BlockSpec((half, rows, width), lambda i, t: (0, 0, 0))

    in_vmem = pl.BlockSpec(memory_space=pltpu.VMEM)
    in_hbm = pl.BlockSpec(memory_space=pltpu.HBM)
    ranks = jnp.stack([r ^ k for k in range(4)])

    def pick(name, *groups):
        places = [(k, h, o, i) for o, group in enumerate(groups) for i, (k, h) in enumerate(group)]
        return pl.pallas_call(
            functools.partial(pick_kernel, places),
            out_shape=[jax.ShapeDtypeStruct((len(group), half, rows, width), BF16) for group in groups],
            grid_spec=pltpu.PrefetchScalarGridSpec(
                num_scalar_prefetch=1,
                grid=(1,),
                in_specs=[in_hbm],
                out_specs=[in_vmem] * len(groups),
                scratch_shapes=[pltpu.SemaphoreType.DMA((len(places),))],
            ),
            compiler_params=params,
            name=name,
        )(ranks, parts)

    def opposite(h):
        return lax.dynamic_slice(parts, (r ^ 2, h, 0, 0, 0), (1, 1, half, rows, width))[0, 0]

    relayed_a = lax.ppermute(opposite(0), "rep", swap1)
    relayed_b = lax.ppermute(opposite(1), "rep", swap3)
    send_a, send_b, kept_a, kept_b, own = pick(
        "pick", [(1, 0)], [(3, 1)], [(3, 0)], [(1, 1)], [(0, 0), (0, 1)]
    )
    direct_a = lax.ppermute(send_a, "rep", swap1)
    direct_b = lax.ppermute(send_b, "rep", swap3)

    def relay(kept, relayed):
        return pl.pallas_call(
            relay_kernel,
            in_specs=[in_vmem] * 2,
            out_specs=in_vmem,
            out_shape=half_shape,
            compiler_params=params,
            name="relay",
        )(kept, relayed)

    second_a = lax.ppermute(relay(kept_a, relayed_a), "rep", swap3)
    second_b = lax.ppermute(relay(kept_b, relayed_b), "rep", swap1)
    presum = pl.pallas_call(
        presum_kernel,
        in_specs=[in_vmem] * 3,
        out_specs=in_vmem,
        out_shape=jax.ShapeDtypeStruct((per_row, rows, width), F32),
        compiler_params=params,
        name="presum",
    )(own, direct_a, direct_b)

    outgoing = pl.pallas_call(
        pack_kernel,
        out_shape=jax.ShapeDtypeStruct((fsdp, capacity, rows, width), BF16),
        grid_spec=pltpu.PrefetchScalarGridSpec(
            num_scalar_prefetch=1,
            grid=(1,),
            in_specs=[pl.BlockSpec((per_row, rows, width), lambda i, t: (0, 0, 0)), half_spec, half_spec],
            out_specs=pl.BlockSpec((fsdp, capacity, rows, width), lambda i, t: (0, 0, 0, 0)),
            scratch_shapes=[pltpu.VMEM((per_row + 1, rows, width), F32)],
        ),
        compiler_params=params,
        name="pack",
    )(block_of, presum, second_a, second_b)

    arrived = lax.all_to_all(outgoing, "fsdp", split_axis=0, concat_axis=0, tiled=True)

    anywhere = pl.BlockSpec(memory_space=pl.ANY)
    factors = jax.ShapeDtypeStruct((capacity, order, order), F32)
    new_left, new_right, slot_update = pl.pallas_call(
        owner_kernel,
        in_specs=[in_vmem, in_vmem, in_vmem],
        out_specs=[anywhere, anywhere, in_vmem],
        out_shape=[factors, factors, jax.ShapeDtypeStruct((fsdp, capacity, rows, width), BF16)],
        scratch_shapes=[
            pltpu.VMEM((capacity, order, order), F32),
            pltpu.VMEM((capacity, order, order), F32),
            pltpu.SemaphoreType.DMA((2 * capacity,)),
        ],
        compiler_params=params,
        name="owner",
    )(arrived, left_factors[0, 0], right_factors[0, 0])

    returned = lax.all_to_all(slot_update, "fsdp", split_axis=0, concat_axis=0, tiled=True)

    mine_a, mine_b = pl.pallas_call(
        unpack_kernel,
        out_shape=[half_shape] * 2,
        grid_spec=pltpu.PrefetchScalarGridSpec(
            num_scalar_prefetch=1,
            grid=(1,),
            in_specs=[pl.BlockSpec((fsdp * capacity, rows, width), lambda i, t: (0, 0, 0))],
            out_specs=[half_spec, half_spec],
        ),
        compiler_params=params,
        name="unpack",
    )(slot_of, returned.reshape(fsdp * capacity, rows, width))

    plus = [(i, (i + 1) % reps) for i in range(reps)]
    minus = [(i, (i - 1) % reps) for i in range(reps)]
    left_a = lax.ppermute(mine_a, "rep", plus)
    right_b = lax.ppermute(mine_b, "rep", minus)
    left_b = lax.ppermute(mine_b, "rep", plus)
    right_a = lax.ppermute(mine_a, "rep", minus)
    far_a = lax.ppermute(left_a, "rep", plus)
    far_b = lax.ppermute(right_b, "rep", minus)
    update_shape = jax.ShapeDtypeStruct((reps, 2, half, rows, width), BF16)
    row_spec = pl.BlockSpec((1, 2, half, rows, width), lambda i, t: (t[i], 0, 0, 0, 0))
    near = pl.pallas_call(
        place_near_kernel,
        out_shape=update_shape,
        grid_spec=pltpu.PrefetchScalarGridSpec(
            num_scalar_prefetch=1, grid=(3,), in_specs=[half_spec] * 6, out_specs=row_spec
        ),
        compiler_params=params,
        name="place_near",
    )(jnp.stack([r, (r + 3) % reps, (r + 1) % reps]), mine_a, mine_b, left_a, left_b, right_a, right_b)
    update = pl.pallas_call(
        place_far_kernel,
        out_shape=update_shape,
        grid_spec=pltpu.PrefetchScalarGridSpec(
            num_scalar_prefetch=1, grid=(1,), in_specs=[half_spec, half_spec, anywhere], out_specs=row_spec
        ),
        input_output_aliases={3: 0},
        compiler_params=params,
        name="place_far",
    )(((r + 2) % reps)[None], far_a, far_b, near)
    return (update.reshape(reps * per_row, rows, width), new_left[None, None], new_right[None, None])


def solution(mesh):
    in_specs = (
        P("rep", None, "fsdp", None),
        P("rep", "fsdp", None, None, None),
        P("rep", "fsdp", None, None, None),
        P(),
    )
    out_specs = (
        P(None, "fsdp", None),
        P("rep", "fsdp", None, None, None),
        P("rep", "fsdp", None, None, None),
    )
    return jax.shard_map(shards, mesh=mesh, in_specs=in_specs, out_specs=out_specs, check_vma=False)
```

```python
import functools

import jax
import jax.numpy as jnp
from jax import lax
from jax.experimental import pallas as pl
from jax.experimental.pallas import tpu as pltpu
from jax.sharding import PartitionSpec as P

BF16 = jnp.bfloat16
F32 = jnp.float32
VMEM_BYTES = 36 * 1024 * 1024


def routing_tables(owner_ids, fsdp_count, capacity):
    count = owner_ids.shape[0]
    position = jnp.arange(count, dtype=jnp.int32)
    same_owner = owner_ids[:, None] == owner_ids[None, :]
    earlier = position[None, :] < position[:, None]
    slot_rank = jnp.sum((same_owner & earlier).astype(jnp.int32), axis=1)
    slot_of = owner_ids * capacity + slot_rank
    slots = jnp.arange(fsdp_count * capacity, dtype=jnp.int32)
    holds = slot_of[None, :] == slots[:, None]
    block_of = count + jnp.sum(jnp.where(holds, position[None, :] - count, 0), axis=1)
    return block_of.astype(jnp.int32), slot_of.astype(jnp.int32)


def pick_kernel(places, table, parts, *refs):
    outs, sems = refs[:-1], refs[-1]
    copies = []
    for i, (k, h, target, row) in enumerate(places):
        copies.append(pltpu.make_async_copy(parts.at[table[k], h], outs[target].at[row], sems.at[i]))
    for copy in copies:
        copy.start()
    for copy in copies:
        copy.wait()


def relay_kernel(kept, relayed, out):
    out[...] = (kept[0].astype(F32) + relayed[...].astype(F32)).astype(BF16)


def presum_kernel(own, direct_a, direct_b, out):
    half = direct_a.shape[1]
    for k, direct in enumerate((direct_a, direct_b)):
        out[k * half : (k + 1) * half] = own[k].astype(F32) + direct[0].astype(F32)


def pack_kernel(table, presum, second_a, second_b, out, held):
    half = second_a.shape[0]
    count = 2 * half
    for k, second in enumerate((second_a, second_b)):
        rows = slice(k * half, (k + 1) * half)
        held[rows] = presum[rows] + second[...].astype(F32)
    held[count] = jnp.zeros(held.shape[1:], F32)
    owners, capacity = out.shape[0], out.shape[1]

    def move(o, carry):
        for s in range(capacity):
            out[o, s] = held[table[o * capacity + s]].astype(BF16)
        return carry

    lax.fori_loop(0, owners, move, 0, unroll=4)


def dot(a, b, ca=1, cb=0):
    return lax.dot_general(a, b, (((ca,), (cb,)), ((), ())), preferred_element_type=F32)


def inverse_roots(matrices, identity):
    ys = [m * lax.rsqrt(jnp.sum(m * m) + 1e-06) for m in matrices]
    ybs = [y.astype(BF16) for y in ys]
    y2s = [dot(b, b) for b in ybs]
    ss = [2.25 * y - 1.5 * y2 + 0.25 * dot(y2.astype(BF16), b) for y, y2, b in zip(ys, y2s, ybs)]
    sbs = [s.astype(BF16) for s in ss]
    s2s = [dot(s, s) for s in sbs]
    qs = [
        -2.4375 * s + 1.6875 * s2 + dot(s2.astype(BF16), (0.0625 * s2 - 0.5625 * s).astype(BF16))
        for s, s2 in zip(ss, s2s)
    ]
    zs = [
        3.375 * identity + 1.5 * q - 1.125 * y - 0.5 * dot(b, q.astype(BF16)) for q, y, b in zip(qs, ys, ybs)
    ]
    return [z.astype(BF16) for z in zs]


def owner_kernel(arrived, left, right, new_left, new_right, out, held_left, held_right, sems):
    capacity, n = left.shape[0], left.shape[1]
    row = lax.broadcasted_iota(jnp.int32, (n, n), 0)
    col = lax.broadcasted_iota(jnp.int32, (n, n), 1)
    identity = (row == col).astype(F32)
    copies, grads, norms, factors = [], [], [], []
    for s in range(capacity):
        wide = arrived[:, s].astype(F32).reshape(n, n)
        grad = wide.astype(BF16)
        turned = grad.T
        new = (
            0.9 * left[s] + 0.1 * dot(grad, grad, 1, 1),
            0.9 * right[s] + 0.1 * dot(turned, turned, 1, 1),
        )
        for k, (held, target) in enumerate(((held_left, new_left), (held_right, new_right))):
            held[s] = new[k]
            copies.append(pltpu.make_async_copy(held.at[s], target.at[s], sems.at[2 * s + k]))
            copies[-1].start()
        grads.append(grad)
        norms.append(jnp.sum(wide * wide))
        factors.append(new)
    for s in range(capacity):
        root_left, root_right = inverse_roots(factors[s], identity)
        half = dot(root_left, grads[s]).astype(BF16)
        raw = dot(half, root_right)
        factor = jnp.sqrt(norms[s]) * lax.rsqrt(jnp.sum(raw * raw) + 1e-06)
        out[:, s] = (raw * factor).reshape(out.shape[0], out.shape[2], out.shape[3]).astype(BF16)
    for copy in copies:
        copy.wait()


def unpack_kernel(table, slots, out_a, out_b):
    half = out_a.shape[0]

    def move(j, carry):
        out_a[j] = slots[table[j]]
        out_b[j] = slots[table[half + j]]
        return carry

    lax.fori_loop(0, half, move, 0, unroll=4)


def place_kernel(places, table, *refs):
    parts, out, sems = refs[: len(places)], refs[-2], refs[-1]
    copies = [
        pltpu.make_async_copy(part, out.at[table[k], h], sems.at[i])
        for i, (part, (k, h)) in enumerate(zip(parts, places))
    ]
    for copy in copies:
        copy.start()
    for copy in copies:
        copy.wait()


def shards(grads, left_factors, right_factors, owners):
    reps = lax.axis_size("rep")
    fsdp = lax.axis_size("fsdp")
    r = lax.axis_index("rep").astype(jnp.int32)
    rows, width = grads.shape[2], grads.shape[3]
    capacity, order = left_factors.shape[2], left_factors.shape[3]
    per_row = grads.shape[1] // reps
    half = per_row // 2
    own_owners = lax.dynamic_index_in_dim(owners[:, :, 0], r, 0, keepdims=False)
    block_of, slot_of = routing_tables(own_owners, fsdp, capacity)

    swap1 = [(i, i ^ 1) for i in range(reps)]
    swap3 = [(i, i ^ 3) for i in range(reps)]
    parts = grads.reshape(reps, 2, half, rows, width)
    params = pltpu.CompilerParams(vmem_limit_bytes=VMEM_BYTES)
    half_shape = jax.ShapeDtypeStruct((half, rows, width), BF16)

    in_vmem = pl.BlockSpec(memory_space=pltpu.VMEM)
    in_hbm = pl.BlockSpec(memory_space=pltpu.HBM)
    ranks = jnp.stack([r ^ k for k in range(4)])

    def pick(name, *groups):
        places = [(k, h, o, i) for o, group in enumerate(groups) for i, (k, h) in enumerate(group)]
        return pl.pallas_call(
            functools.partial(pick_kernel, places),
            out_shape=[jax.ShapeDtypeStruct((len(group), half, rows, width), BF16) for group in groups],
            grid_spec=pltpu.PrefetchScalarGridSpec(
                num_scalar_prefetch=1,
                grid=(1,),
                in_specs=[in_hbm],
                out_specs=[in_vmem] * len(groups),
                scratch_shapes=[pltpu.SemaphoreType.DMA((len(places),))],
            ),
            compiler_params=params,
            name=name,
        )(ranks, parts)

    def opposite(h):
        return lax.dynamic_slice(parts, (r ^ 2, h, 0, 0, 0), (1, 1, half, rows, width))[0, 0]

    relayed_a = lax.ppermute(opposite(0), "rep", swap1)
    relayed_b = lax.ppermute(opposite(1), "rep", swap3)
    send_a, send_b, kept_a, kept_b, own = pick(
        "pick", [(1, 0)], [(3, 1)], [(3, 0)], [(1, 1)], [(0, 0), (0, 1)]
    )
    direct_a = lax.ppermute(send_a, "rep", swap1)
    direct_b = lax.ppermute(send_b, "rep", swap3)

    def relay(kept, relayed):
        return pl.pallas_call(
            relay_kernel,
            in_specs=[in_vmem] * 2,
            out_specs=in_vmem,
            out_shape=half_shape,
            compiler_params=params,
            name="relay",
        )(kept, relayed)

    second_a = lax.ppermute(relay(kept_a, relayed_a), "rep", swap3)
    second_b = lax.ppermute(relay(kept_b, relayed_b), "rep", swap1)
    presum = pl.pallas_call(
        presum_kernel,
        in_specs=[in_vmem] * 3,
        out_specs=in_vmem,
        out_shape=jax.ShapeDtypeStruct((per_row, rows, width), F32),
        compiler_params=params,
        name="presum",
    )(own, direct_a, direct_b)

    outgoing = pl.pallas_call(
        pack_kernel,
        out_shape=jax.ShapeDtypeStruct((fsdp, capacity, rows, width), BF16),
        grid_spec=pltpu.PrefetchScalarGridSpec(
            num_scalar_prefetch=1,
            grid=(1,),
            in_specs=[in_vmem] * 3,
            out_specs=in_vmem,
            scratch_shapes=[pltpu.VMEM((per_row + 1, rows, width), F32)],
        ),
        compiler_params=params,
        name="pack",
    )(block_of, presum, second_a, second_b)

    arrived = lax.all_to_all(outgoing, "fsdp", split_axis=0, concat_axis=0, tiled=True)

    anywhere = pl.BlockSpec(memory_space=pl.ANY)
    factors = jax.ShapeDtypeStruct((capacity, order, order), F32)
    new_left, new_right, slot_update = pl.pallas_call(
        owner_kernel,
        in_specs=[in_vmem, in_vmem, in_vmem],
        out_specs=[anywhere, anywhere, in_vmem],
        out_shape=[factors, factors, jax.ShapeDtypeStruct((fsdp, capacity, rows, width), BF16)],
        scratch_shapes=[
            pltpu.VMEM((capacity, order, order), F32),
            pltpu.VMEM((capacity, order, order), F32),
            pltpu.SemaphoreType.DMA((2 * capacity,)),
        ],
        compiler_params=params,
        name="owner",
    )(arrived, left_factors[0, 0], right_factors[0, 0])

    returned = lax.all_to_all(slot_update, "fsdp", split_axis=0, concat_axis=0, tiled=True)

    mine_a, mine_b = pl.pallas_call(
        unpack_kernel,
        out_shape=[half_shape] * 2,
        grid_spec=pltpu.PrefetchScalarGridSpec(
            num_scalar_prefetch=1,
            grid=(1,),
            in_specs=[in_vmem],
            out_specs=[in_vmem, in_vmem],
        ),
        compiler_params=params,
        name="unpack",
    )(slot_of, returned.reshape(fsdp * capacity, rows, width))

    plus = [(i, (i + 1) % reps) for i in range(reps)]
    minus = [(i, (i - 1) % reps) for i in range(reps)]
    left_a = lax.ppermute(mine_a, "rep", plus)
    right_b = lax.ppermute(mine_b, "rep", minus)
    left_b = lax.ppermute(mine_b, "rep", plus)
    right_a = lax.ppermute(mine_a, "rep", minus)
    far_a = lax.ppermute(left_a, "rep", plus)
    far_b = lax.ppermute(right_b, "rep", minus)
    update_shape = jax.ShapeDtypeStruct((reps, 2, half, rows, width), BF16)
    turns = jnp.stack([(r + k) % reps for k in range(4)])

    def place(name, places, values, before=None):
        held = [] if before is None else [before]
        return pl.pallas_call(
            functools.partial(place_kernel, places),
            out_shape=update_shape,
            grid_spec=pltpu.PrefetchScalarGridSpec(
                num_scalar_prefetch=1,
                grid=(1,),
                in_specs=[in_vmem] * len(values) + [anywhere] * len(held),
                out_specs=anywhere,
                scratch_shapes=[pltpu.SemaphoreType.DMA((len(places),))],
            ),
            input_output_aliases={len(values) + 1: 0} if held else {},
            compiler_params=params,
            name=name,
        )(turns, *values, *held)

    update = place("place_first", [(0, 0), (0, 1), (3, 0), (1, 1)], [mine_a, mine_b, left_a, right_b])
    update = place("place_second", [(3, 1), (1, 0)], [left_b, right_a], update)
    update = place("place_far", [(2, 0), (2, 1)], [far_a, far_b], update)
    return (update.reshape(reps * per_row, rows, width), new_left[None, None], new_right[None, None])


def solution(mesh):
    in_specs = (
        P("rep", None, "fsdp", None),
        P("rep", "fsdp", None, None, None),
        P("rep", "fsdp", None, None, None),
        P(),
    )
    out_specs = (
        P(None, "fsdp", None),
        P("rep", "fsdp", None, None, None),
        P("rep", "fsdp", None, None, None),
    )
    return jax.shard_map(shards, mesh=mesh, in_specs=in_specs, out_specs=out_specs, check_vma=False)
```

```python
import functools

import jax
import jax.numpy as jnp
from jax import lax
from jax.experimental import pallas as pl
from jax.experimental.pallas import tpu as pltpu
from jax.sharding import PartitionSpec as P

BF16 = jnp.bfloat16
F32 = jnp.float32
VMEM_BYTES = 36 * 1024 * 1024


def slots_of_blocks(owner_ids, capacity):
    position = jnp.arange(owner_ids.shape[0], dtype=jnp.int32)
    same_owner = owner_ids[:, None] == owner_ids[None, :]
    earlier = position[None, :] < position[:, None]
    slot_rank = jnp.sum((same_owner & earlier).astype(jnp.int32), axis=1)
    return owner_ids * capacity + slot_rank


def pick_kernel(places, table, parts, *refs):
    outs, sems = refs[:-1], refs[-1]
    copies = []
    for i, (k, h, target, row) in enumerate(places):
        copies.append(pltpu.make_async_copy(parts.at[table[k], h], outs[target].at[row], sems.at[i]))
    for copy in copies:
        copy.start()
    for copy in copies:
        copy.wait()


def relay_kernel(kept, relayed, out):
    out[...] = (kept[0].astype(F32) + relayed[...].astype(F32)).astype(BF16)


def presum_kernel(own, direct_a, direct_b, out):
    half = direct_a.shape[1]
    for k, direct in enumerate((direct_a, direct_b)):
        out[k * half : (k + 1) * half] = own[k].astype(F32) + direct[0].astype(F32)


def pack_kernel(table, presum, second_a, second_b, out):
    half = second_a.shape[0]
    out[...] = jnp.zeros(out.shape, out.dtype)
    for k, second in enumerate((second_a, second_b)):

        def move(j, carry, k=k, second=second):
            total = presum[k * half + j] + second[j].astype(F32)
            out[table[k * half + j]] = total.astype(BF16)
            return carry

        lax.fori_loop(0, half, move, 0, unroll=8)


def dot(a, b, ca=1, cb=0):
    return lax.dot_general(a, b, (((ca,), (cb,)), ((), ())), preferred_element_type=F32)


def inverse_roots(matrices, identity):
    ys = [m * lax.rsqrt(jnp.sum(m * m) + 1e-06) for m in matrices]
    ybs = [y.astype(BF16) for y in ys]
    y2s = [dot(b, b) for b in ybs]
    ss = [2.25 * y - 1.5 * y2 + 0.25 * dot(y2.astype(BF16), b) for y, y2, b in zip(ys, y2s, ybs)]
    sbs = [s.astype(BF16) for s in ss]
    s2s = [dot(s, s) for s in sbs]
    qs = [
        -2.4375 * s + 1.6875 * s2 + dot(s2.astype(BF16), (0.0625 * s2 - 0.5625 * s).astype(BF16))
        for s, s2 in zip(ss, s2s)
    ]
    zs = [
        3.375 * identity + 1.5 * q - 1.125 * y - 0.5 * dot(b, q.astype(BF16)) for q, y, b in zip(qs, ys, ybs)
    ]
    return [z.astype(BF16) for z in zs]


def owner_kernel(arrived, left, right, new_left, new_right, out, held_left, held_right, sems):
    capacity, n = left.shape[0], left.shape[1]
    row = lax.broadcasted_iota(jnp.int32, (n, n), 0)
    col = lax.broadcasted_iota(jnp.int32, (n, n), 1)
    identity = (row == col).astype(F32)
    copies, grads, norms, factors = [], [], [], []
    for s in range(capacity):
        wide = arrived[:, s].astype(F32).reshape(n, n)
        grad = wide.astype(BF16)
        turned = grad.T
        new = (
            0.9 * left[s] + 0.1 * dot(grad, grad, 1, 1),
            0.9 * right[s] + 0.1 * dot(turned, turned, 1, 1),
        )
        for k, (held, target) in enumerate(((held_left, new_left), (held_right, new_right))):
            held[s] = new[k]
            copies.append(pltpu.make_async_copy(held.at[s], target.at[s], sems.at[2 * s + k]))
            copies[-1].start()
        grads.append(grad)
        norms.append(jnp.sum(wide * wide))
        factors.append(new)
    for s in range(capacity):
        root_left, root_right = inverse_roots(factors[s], identity)
        half = dot(root_left, grads[s]).astype(BF16)
        raw = dot(half, root_right)
        factor = jnp.sqrt(norms[s]) * lax.rsqrt(jnp.sum(raw * raw) + 1e-06)
        out[:, s] = (raw * factor).reshape(out.shape[0], out.shape[2], out.shape[3]).astype(BF16)
    for copy in copies:
        copy.wait()


def unpack_kernel(table, slots, out_a, out_b):
    half = out_a.shape[0]

    def move(j, carry):
        out_a[j] = slots[table[j]]
        out_b[j] = slots[table[half + j]]
        return carry

    lax.fori_loop(0, half, move, 0, unroll=4)


def place_kernel(count, table, *refs):
    parts, out = refs[:count], refs[-1]
    for k, part in enumerate(parts):

        @pl.when(pl.program_id(0) == k)
        def _():
            out[0, 0] = part[...]


def shards(grads, left_factors, right_factors, owners):
    reps = lax.axis_size("rep")
    fsdp = lax.axis_size("fsdp")
    r = lax.axis_index("rep").astype(jnp.int32)
    rows, width = grads.shape[2], grads.shape[3]
    capacity, order = left_factors.shape[2], left_factors.shape[3]
    per_row = grads.shape[1] // reps
    half = per_row // 2
    own_owners = lax.dynamic_index_in_dim(owners[:, :, 0], r, 0, keepdims=False)
    slot_of = slots_of_blocks(own_owners, capacity)

    swap1 = [(i, i ^ 1) for i in range(reps)]
    swap3 = [(i, i ^ 3) for i in range(reps)]
    parts = grads.reshape(reps, 2, half, rows, width)
    params = pltpu.CompilerParams(vmem_limit_bytes=VMEM_BYTES)
    half_shape = jax.ShapeDtypeStruct((half, rows, width), BF16)

    in_vmem = pl.BlockSpec(memory_space=pltpu.VMEM)
    in_hbm = pl.BlockSpec(memory_space=pltpu.HBM)
    ranks = jnp.stack([r ^ k for k in range(4)])

    def pick(name, *groups):
        places = [(k, h, o, i) for o, group in enumerate(groups) for i, (k, h) in enumerate(group)]
        return pl.pallas_call(
            functools.partial(pick_kernel, places),
            out_shape=[jax.ShapeDtypeStruct((len(group), half, rows, width), BF16) for group in groups],
            grid_spec=pltpu.PrefetchScalarGridSpec(
                num_scalar_prefetch=1,
                grid=(1,),
                in_specs=[in_hbm],
                out_specs=[in_vmem] * len(groups),
                scratch_shapes=[pltpu.SemaphoreType.DMA((len(places),))],
            ),
            compiler_params=params,
            name=name,
        )(ranks, parts)

    def opposite(h):
        return lax.dynamic_slice(parts, (r ^ 2, h, 0, 0, 0), (1, 1, half, rows, width))[0, 0]

    relayed_a = lax.ppermute(opposite(0), "rep", swap1)
    relayed_b = lax.ppermute(opposite(1), "rep", swap3)
    send_a, send_b, kept_a, kept_b, own = pick(
        "pick", [(1, 0)], [(3, 1)], [(3, 0)], [(1, 1)], [(0, 0), (0, 1)]
    )
    direct_a = lax.ppermute(send_a, "rep", swap1)
    direct_b = lax.ppermute(send_b, "rep", swap3)

    def relay(kept, relayed):
        return pl.pallas_call(
            relay_kernel,
            in_specs=[in_vmem] * 2,
            out_specs=in_vmem,
            out_shape=half_shape,
            compiler_params=params,
            name="relay",
        )(kept, relayed)

    second_a = lax.ppermute(relay(kept_a, relayed_a), "rep", swap3)
    second_b = lax.ppermute(relay(kept_b, relayed_b), "rep", swap1)
    presum = pl.pallas_call(
        presum_kernel,
        in_specs=[in_vmem] * 3,
        out_specs=in_vmem,
        out_shape=jax.ShapeDtypeStruct((per_row, rows, width), F32),
        compiler_params=params,
        name="presum",
    )(own, direct_a, direct_b)

    outgoing = pl.pallas_call(
        pack_kernel,
        out_shape=jax.ShapeDtypeStruct((fsdp * capacity, rows, width), BF16),
        grid_spec=pltpu.PrefetchScalarGridSpec(
            num_scalar_prefetch=1, grid=(1,), in_specs=[in_vmem] * 3, out_specs=in_vmem
        ),
        compiler_params=params,
        name="pack",
    )(slot_of, presum, second_a, second_b).reshape(fsdp, capacity, rows, width)

    arrived = lax.all_to_all(outgoing, "fsdp", split_axis=0, concat_axis=0, tiled=True)

    anywhere = pl.BlockSpec(memory_space=pl.ANY)
    factors = jax.ShapeDtypeStruct((capacity, order, order), F32)
    new_left, new_right, slot_update = pl.pallas_call(
        owner_kernel,
        in_specs=[in_vmem, in_vmem, in_vmem],
        out_specs=[anywhere, anywhere, in_vmem],
        out_shape=[factors, factors, jax.ShapeDtypeStruct((fsdp, capacity, rows, width), BF16)],
        scratch_shapes=[
            pltpu.VMEM((capacity, order, order), F32),
            pltpu.VMEM((capacity, order, order), F32),
            pltpu.SemaphoreType.DMA((2 * capacity,)),
        ],
        compiler_params=params,
        name="owner",
    )(arrived, left_factors[0, 0], right_factors[0, 0])

    returned = lax.all_to_all(slot_update, "fsdp", split_axis=0, concat_axis=0, tiled=True)

    mine_a, mine_b = pl.pallas_call(
        unpack_kernel,
        out_shape=[half_shape] * 2,
        grid_spec=pltpu.PrefetchScalarGridSpec(
            num_scalar_prefetch=1,
            grid=(1,),
            in_specs=[in_vmem],
            out_specs=[in_vmem, in_vmem],
        ),
        compiler_params=params,
        name="unpack",
    )(slot_of, returned.reshape(fsdp * capacity, rows, width))

    plus = [(i, (i + 1) % reps) for i in range(reps)]
    minus = [(i, (i - 1) % reps) for i in range(reps)]
    left_a = lax.ppermute(mine_a, "rep", plus)
    right_b = lax.ppermute(mine_b, "rep", minus)
    left_b = lax.ppermute(mine_b, "rep", plus)
    right_a = lax.ppermute(mine_a, "rep", minus)
    far_a = lax.ppermute(left_a, "rep", plus)
    far_b = lax.ppermute(right_b, "rep", minus)
    update_shape = jax.ShapeDtypeStruct((reps, 2, half, rows, width), BF16)

    def place(name, places, values, before=None):
        held = [] if before is None else [before]
        count = len(values)
        table = jnp.stack([(r + k) % reps for k, _ in places] + [jnp.int32(h) for _, h in places])
        return pl.pallas_call(
            functools.partial(place_kernel, count),
            out_shape=update_shape,
            grid_spec=pltpu.PrefetchScalarGridSpec(
                num_scalar_prefetch=1,
                grid=(count,),
                in_specs=[in_vmem] * count + [anywhere] * len(held),
                out_specs=pl.BlockSpec((1, 1, half, rows, width), lambda i, t: (t[i], t[count + i], 0, 0, 0)),
            ),
            input_output_aliases={count + 1: 0} if held else {},
            compiler_params=params,
            name=name,
        )(table, *values, *held)

    update = place("place_first", [(0, 0), (0, 1), (3, 0), (1, 1)], [mine_a, mine_b, left_a, right_b])
    update = place("place_second", [(3, 1), (1, 0)], [left_b, right_a], update)
    update = place("place_far", [(2, 0), (2, 1)], [far_a, far_b], update)
    return (update.reshape(reps * per_row, rows, width), new_left[None, None], new_right[None, None])


def solution(mesh):
    in_specs = (
        P("rep", None, "fsdp", None),
        P("rep", "fsdp", None, None, None),
        P("rep", "fsdp", None, None, None),
        P(),
    )
    out_specs = (
        P(None, "fsdp", None),
        P("rep", "fsdp", None, None, None),
        P("rep", "fsdp", None, None, None),
    )
    return jax.shard_map(shards, mesh=mesh, in_specs=in_specs, out_specs=out_specs, check_vma=False)
```

```python
import functools

import jax
import jax.numpy as jnp
from jax import lax
from jax.experimental import pallas as pl
from jax.experimental.pallas import tpu as pltpu
from jax.sharding import PartitionSpec as P

BF16 = jnp.bfloat16
F32 = jnp.float32
VMEM_BYTES = 36 * 1024 * 1024


def slots_of_blocks(owner_ids, capacity):
    position = jnp.arange(owner_ids.shape[0], dtype=jnp.int32)
    same_owner = owner_ids[:, None] == owner_ids[None, :]
    earlier = position[None, :] < position[:, None]
    slot_rank = jnp.sum((same_owner & earlier).astype(jnp.int32), axis=1)
    return owner_ids * capacity + slot_rank


def pick_kernel(places, table, parts, *refs):
    outs, sems = refs[:-1], refs[-1]
    copies = []
    for i, (k, h, target, row) in enumerate(places):
        copies.append(pltpu.make_async_copy(parts.at[table[k], h], outs[target].at[row], sems.at[i]))
    for copy in copies:
        copy.start()
    for copy in copies:
        copy.wait()


def relay_kernel(kept, relayed, out):
    out[...] = (kept[0].astype(F32) + relayed[...].astype(F32)).astype(BF16)


def presum_kernel(own, direct_a, direct_b, out):
    half = direct_a.shape[1]
    for k, direct in enumerate((direct_a, direct_b)):
        out[k * half : (k + 1) * half] = own[k].astype(F32) + direct[0].astype(F32)


def pack_kernel(table, presum, second_a, second_b, out):
    half = second_a.shape[0]
    out[...] = jnp.zeros(out.shape, out.dtype)
    for k, second in enumerate((second_a, second_b)):

        def move(j, carry, k=k, second=second):
            total = presum[k * half + j] + second[j].astype(F32)
            out[table[k * half + j]] = total.astype(BF16)
            return carry

        lax.fori_loop(0, half, move, 0, unroll=8)


def dot(a, b, ca=1, cb=0):
    return lax.dot_general(a, b, (((ca,), (cb,)), ((), ())), preferred_element_type=F32)


def inverse_roots(matrices, identity):
    ys = [m * lax.rsqrt(jnp.sum(m * m) + 1e-06) for m in matrices]
    ybs = [y.astype(BF16) for y in ys]
    y2s = [dot(b, b) for b in ybs]
    ss = [2.25 * y - 1.5 * y2 + 0.25 * dot(y2.astype(BF16), b) for y, y2, b in zip(ys, y2s, ybs)]
    sbs = [s.astype(BF16) for s in ss]
    s2s = [dot(s, s) for s in sbs]
    qs = [
        -2.4375 * s + 1.6875 * s2 + dot(s2.astype(BF16), (0.0625 * s2 - 0.5625 * s).astype(BF16))
        for s, s2 in zip(ss, s2s)
    ]
    zs = [
        3.375 * identity + 1.5 * q - 1.125 * y - 0.5 * dot(b, q.astype(BF16)) for q, y, b in zip(qs, ys, ybs)
    ]
    return [z.astype(BF16) for z in zs]


def owner_kernel(arrived, left, right, new_left, new_right, out, held_left, held_right, sems):
    capacity, n = left.shape[0], left.shape[1]
    row = lax.broadcasted_iota(jnp.int32, (n, n), 0)
    col = lax.broadcasted_iota(jnp.int32, (n, n), 1)
    identity = (row == col).astype(F32)
    copies, grads, norms, factors = [], [], [], []
    for s in range(capacity):
        wide = arrived[:, s].astype(F32).reshape(n, n)
        grad = wide.astype(BF16)
        turned = grad.T
        new = (
            0.9 * left[s] + 0.1 * dot(grad, grad, 1, 1),
            0.9 * right[s] + 0.1 * dot(turned, turned, 1, 1),
        )
        for k, (held, target) in enumerate(((held_left, new_left), (held_right, new_right))):
            held[s] = new[k]
            copies.append(pltpu.make_async_copy(held.at[s], target.at[s], sems.at[2 * s + k]))
            copies[-1].start()
        grads.append(grad)
        norms.append(jnp.sum(wide * wide))
        factors.append(new)
    for s in range(capacity):
        root_left, root_right = inverse_roots(factors[s], identity)
        half = dot(root_left, grads[s]).astype(BF16)
        raw = dot(half, root_right)
        factor = jnp.sqrt(norms[s]) * lax.rsqrt(jnp.sum(raw * raw) + 1e-06)
        out[:, s] = (raw * factor).reshape(out.shape[0], out.shape[2], out.shape[3]).astype(BF16)
    for copy in copies:
        copy.wait()


def unpack_kernel(table, slots, out_a, out_b):
    half = out_a.shape[0]

    def move(j, carry):
        out_a[j] = slots[table[j]]
        out_b[j] = slots[table[half + j]]
        return carry

    lax.fori_loop(0, half, move, 0, unroll=4)


def place_kernel(steps, table, *refs):
    out = refs[-1]
    for k, step in enumerate(steps):

        @pl.when(pl.program_id(0) == k)
        def _():
            for i, part in enumerate(step):
                out[0, i] = refs[part][...]


def shards(grads, left_factors, right_factors, owners):
    reps = lax.axis_size("rep")
    fsdp = lax.axis_size("fsdp")
    r = lax.axis_index("rep").astype(jnp.int32)
    rows, width = grads.shape[2], grads.shape[3]
    capacity, order = left_factors.shape[2], left_factors.shape[3]
    per_row = grads.shape[1] // reps
    half = per_row // 2
    own_owners = lax.dynamic_index_in_dim(owners[:, :, 0], r, 0, keepdims=False)
    slot_of = slots_of_blocks(own_owners, capacity)

    swap1 = [(i, i ^ 1) for i in range(reps)]
    swap3 = [(i, i ^ 3) for i in range(reps)]
    parts = grads.reshape(reps, 2, half, rows, width)
    params = pltpu.CompilerParams(vmem_limit_bytes=VMEM_BYTES)
    half_shape = jax.ShapeDtypeStruct((half, rows, width), BF16)

    in_vmem = pl.BlockSpec(memory_space=pltpu.VMEM)
    in_hbm = pl.BlockSpec(memory_space=pltpu.HBM)
    ranks = jnp.stack([r ^ k for k in range(4)])

    def pick(name, *groups):
        places = [(k, h, o, i) for o, group in enumerate(groups) for i, (k, h) in enumerate(group)]
        return pl.pallas_call(
            functools.partial(pick_kernel, places),
            out_shape=[jax.ShapeDtypeStruct((len(group), half, rows, width), BF16) for group in groups],
            grid_spec=pltpu.PrefetchScalarGridSpec(
                num_scalar_prefetch=1,
                grid=(1,),
                in_specs=[in_hbm],
                out_specs=[in_vmem] * len(groups),
                scratch_shapes=[pltpu.SemaphoreType.DMA((len(places),))],
            ),
            compiler_params=params,
            name=name,
        )(ranks, parts)

    def opposite(h):
        return lax.dynamic_slice(parts, (r ^ 2, h, 0, 0, 0), (1, 1, half, rows, width))[0, 0]

    relayed_a = lax.ppermute(opposite(0), "rep", swap1)
    relayed_b = lax.ppermute(opposite(1), "rep", swap3)
    send_a, send_b, kept_a, kept_b, own = pick(
        "pick", [(1, 0)], [(3, 1)], [(3, 0)], [(1, 1)], [(0, 0), (0, 1)]
    )
    direct_a = lax.ppermute(send_a, "rep", swap1)
    direct_b = lax.ppermute(send_b, "rep", swap3)

    def relay(kept, relayed):
        return pl.pallas_call(
            relay_kernel,
            in_specs=[in_vmem] * 2,
            out_specs=in_vmem,
            out_shape=half_shape,
            compiler_params=params,
            name="relay",
        )(kept, relayed)

    second_a = lax.ppermute(relay(kept_a, relayed_a), "rep", swap3)
    second_b = lax.ppermute(relay(kept_b, relayed_b), "rep", swap1)
    presum = pl.pallas_call(
        presum_kernel,
        in_specs=[in_vmem] * 3,
        out_specs=in_vmem,
        out_shape=jax.ShapeDtypeStruct((per_row, rows, width), F32),
        compiler_params=params,
        name="presum",
    )(own, direct_a, direct_b)

    outgoing = pl.pallas_call(
        pack_kernel,
        out_shape=jax.ShapeDtypeStruct((fsdp * capacity, rows, width), BF16),
        grid_spec=pltpu.PrefetchScalarGridSpec(
            num_scalar_prefetch=1, grid=(1,), in_specs=[in_vmem] * 3, out_specs=in_vmem
        ),
        compiler_params=params,
        name="pack",
    )(slot_of, presum, second_a, second_b).reshape(fsdp, capacity, rows, width)

    arrived = lax.all_to_all(outgoing, "fsdp", split_axis=0, concat_axis=0, tiled=True)

    anywhere = pl.BlockSpec(memory_space=pl.ANY)
    factors = jax.ShapeDtypeStruct((capacity, order, order), F32)
    new_left, new_right, slot_update = pl.pallas_call(
        owner_kernel,
        in_specs=[in_vmem, in_vmem, in_vmem],
        out_specs=[anywhere, anywhere, in_vmem],
        out_shape=[factors, factors, jax.ShapeDtypeStruct((fsdp, capacity, rows, width), BF16)],
        scratch_shapes=[
            pltpu.VMEM((capacity, order, order), F32),
            pltpu.VMEM((capacity, order, order), F32),
            pltpu.SemaphoreType.DMA((2 * capacity,)),
        ],
        compiler_params=params,
        name="owner",
    )(arrived, left_factors[0, 0], right_factors[0, 0])

    returned = lax.all_to_all(slot_update, "fsdp", split_axis=0, concat_axis=0, tiled=True)

    mine_a, mine_b = pl.pallas_call(
        unpack_kernel,
        out_shape=[half_shape] * 2,
        grid_spec=pltpu.PrefetchScalarGridSpec(
            num_scalar_prefetch=1,
            grid=(1,),
            in_specs=[in_vmem],
            out_specs=[in_vmem, in_vmem],
        ),
        compiler_params=params,
        name="unpack",
    )(slot_of, returned.reshape(fsdp * capacity, rows, width))

    plus = [(i, (i + 1) % reps) for i in range(reps)]
    minus = [(i, (i - 1) % reps) for i in range(reps)]
    left_a = lax.ppermute(mine_a, "rep", plus)
    right_b = lax.ppermute(mine_b, "rep", minus)
    left_b = lax.ppermute(mine_b, "rep", plus)
    right_a = lax.ppermute(mine_a, "rep", minus)
    far_a = lax.ppermute(left_a, "rep", plus)
    far_b = lax.ppermute(right_b, "rep", minus)
    update_shape = jax.ShapeDtypeStruct((reps, 2, half, rows, width), BF16)

    def place(name, places, steps, values, before=None):
        held = [] if before is None else [before]
        table = jnp.stack([(r + k) % reps for k, _ in places] + [jnp.int32(h) for _, h in places])
        count, size = len(steps), len(steps[0])
        return pl.pallas_call(
            functools.partial(place_kernel, steps),
            out_shape=update_shape,
            grid_spec=pltpu.PrefetchScalarGridSpec(
                num_scalar_prefetch=1,
                grid=(count,),
                in_specs=[in_vmem] * len(values) + [anywhere] * len(held),
                out_specs=pl.BlockSpec(
                    (1, size, half, rows, width), lambda i, t: (t[i], t[count + i], 0, 0, 0)
                ),
            ),
            input_output_aliases={len(values) + 1: 0} if held else {},
            compiler_params=params,
            name=name,
        )(table, *values, *held)

    singles = [(0,), (1,), (2,), (3,)]
    update = place(
        "place_first", [(0, 0), (0, 1), (3, 0), (1, 1)], singles, [mine_a, mine_b, left_a, right_b]
    )
    update = place("place_second", [(3, 1), (1, 0)], singles[:2], [left_b, right_a], update)
    update = place("place_far", [(2, 0)], [(0, 1)], [far_a, far_b], update)
    return (update.reshape(reps * per_row, rows, width), new_left[None, None], new_right[None, None])


def solution(mesh):
    in_specs = (
        P("rep", None, "fsdp", None),
        P("rep", "fsdp", None, None, None),
        P("rep", "fsdp", None, None, None),
        P(),
    )
    out_specs = (
        P(None, "fsdp", None),
        P("rep", "fsdp", None, None, None),
        P("rep", "fsdp", None, None, None),
    )
    return jax.shard_map(shards, mesh=mesh, in_specs=in_specs, out_specs=out_specs, check_vma=False)
```

```python
import functools

import jax
import jax.numpy as jnp
from jax import lax
from jax.experimental import pallas as pl
from jax.experimental.pallas import tpu as pltpu
from jax.sharding import PartitionSpec as P

BF16 = jnp.bfloat16
F32 = jnp.float32
VMEM_BYTES = 36 * 1024 * 1024


def slots_of_blocks(owner_ids, capacity):
    position = jnp.arange(owner_ids.shape[0], dtype=jnp.int32)
    same_owner = owner_ids[:, None] == owner_ids[None, :]
    earlier = position[None, :] < position[:, None]
    slot_rank = jnp.sum((same_owner & earlier).astype(jnp.int32), axis=1)
    return owner_ids * capacity + slot_rank


def pick_kernel(places, table, parts, *refs):
    outs, sems = refs[:-1], refs[-1]
    copies = []
    for i, (k, h, target, row) in enumerate(places):
        copies.append(pltpu.make_async_copy(parts.at[table[0] ^ k, h], outs[target].at[row], sems.at[i]))
    for copy in copies:
        copy.start()
    for copy in copies:
        copy.wait()


def relay_kernel(kept, relayed, out):
    out[...] = (kept[0].astype(F32) + relayed[...].astype(F32)).astype(BF16)


def presum_kernel(own, direct_a, direct_b, out):
    half = direct_a.shape[1]
    for k, direct in enumerate((direct_a, direct_b)):
        out[k * half : (k + 1) * half] = own[k].astype(F32) + direct[0].astype(F32)


def pack_kernel(table, presum, second_a, second_b, out):
    half = second_a.shape[0]
    out[...] = jnp.zeros(out.shape, out.dtype)
    for k, second in enumerate((second_a, second_b)):

        def move(j, carry, k=k, second=second):
            total = presum[k * half + j] + second[j].astype(F32)
            out[table[k * half + j]] = total.astype(BF16)
            return carry

        lax.fori_loop(0, half, move, 0, unroll=8)


def dot(a, b, ca=1, cb=0):
    return lax.dot_general(a, b, (((ca,), (cb,)), ((), ())), preferred_element_type=F32)


def inverse_roots(matrices, identity):
    ys = [m * lax.rsqrt(jnp.sum(m * m) + 1e-06) for m in matrices]
    ybs = [y.astype(BF16) for y in ys]
    y2s = [dot(b, b) for b in ybs]
    ss = [2.25 * y - 1.5 * y2 + 0.25 * dot(y2.astype(BF16), b) for y, y2, b in zip(ys, y2s, ybs)]
    sbs = [s.astype(BF16) for s in ss]
    s2s = [dot(s, s) for s in sbs]
    qs = [
        -2.4375 * s + 1.6875 * s2 + dot(s2.astype(BF16), (0.0625 * s2 - 0.5625 * s).astype(BF16))
        for s, s2 in zip(ss, s2s)
    ]
    zs = [
        3.375 * identity + 1.5 * q - 1.125 * y - 0.5 * dot(b, q.astype(BF16)) for q, y, b in zip(qs, ys, ybs)
    ]
    return [z.astype(BF16) for z in zs]


def owner_kernel(arrived, left, right, new_left, new_right, out, held_left, held_right, sems):
    capacity, n = left.shape[0], left.shape[1]
    row = lax.broadcasted_iota(jnp.int32, (n, n), 0)
    col = lax.broadcasted_iota(jnp.int32, (n, n), 1)
    identity = (row == col).astype(F32)
    copies, grads, norms, factors = [], [], [], []
    for s in range(capacity):
        wide = arrived[:, s].astype(F32).reshape(n, n)
        grad = wide.astype(BF16)
        turned = grad.T
        new = (
            0.9 * left[s] + 0.1 * dot(grad, grad, 1, 1),
            0.9 * right[s] + 0.1 * dot(turned, turned, 1, 1),
        )
        for k, (held, target) in enumerate(((held_left, new_left), (held_right, new_right))):
            held[s] = new[k]
            copies.append(pltpu.make_async_copy(held.at[s], target.at[s], sems.at[2 * s + k]))
            copies[-1].start()
        grads.append(grad)
        norms.append(jnp.sum(wide * wide))
        factors.append(new)
    for s in range(capacity):
        root_left, root_right = inverse_roots(factors[s], identity)
        half = dot(root_left, grads[s]).astype(BF16)
        raw = dot(half, root_right)
        factor = jnp.sqrt(norms[s]) * lax.rsqrt(jnp.sum(raw * raw) + 1e-06)
        out[:, s] = (raw * factor).reshape(out.shape[0], out.shape[2], out.shape[3]).astype(BF16)
    for copy in copies:
        copy.wait()


def unpack_kernel(table, slots, out_a, out_b):
    half = out_a.shape[0]

    def move(j, carry):
        out_a[j] = slots[table[j]]
        out_b[j] = slots[table[half + j]]
        return carry

    lax.fori_loop(0, half, move, 0, unroll=4)


def place_kernel(steps, table, *refs):
    out = refs[-1]
    for k, step in enumerate(steps):

        @pl.when(pl.program_id(0) == k)
        def _():
            for i, part in enumerate(step):
                out[0, i] = refs[part][...]


def shards(grads, left_factors, right_factors, owners):
    reps = lax.axis_size("rep")
    fsdp = lax.axis_size("fsdp")
    r = lax.axis_index("rep").astype(jnp.int32)
    rows, width = grads.shape[2], grads.shape[3]
    capacity, order = left_factors.shape[2], left_factors.shape[3]
    per_row = grads.shape[1] // reps
    half = per_row // 2
    own_owners = lax.dynamic_index_in_dim(owners[:, :, 0], r, 0, keepdims=False)
    slot_of = slots_of_blocks(own_owners, capacity)

    swap1 = [(i, i ^ 1) for i in range(reps)]
    swap3 = [(i, i ^ 3) for i in range(reps)]
    parts = grads.reshape(reps, 2, half, rows, width)
    params = pltpu.CompilerParams(vmem_limit_bytes=VMEM_BYTES)
    half_shape = jax.ShapeDtypeStruct((half, rows, width), BF16)

    in_vmem = pl.BlockSpec(memory_space=pltpu.VMEM)
    in_hbm = pl.BlockSpec(memory_space=pltpu.HBM)

    def pick(name, *groups):
        places = [(k, h, o, i) for o, group in enumerate(groups) for i, (k, h) in enumerate(group)]
        return pl.pallas_call(
            functools.partial(pick_kernel, places),
            out_shape=[jax.ShapeDtypeStruct((len(group), half, rows, width), BF16) for group in groups],
            grid_spec=pltpu.PrefetchScalarGridSpec(
                num_scalar_prefetch=1,
                grid=(1,),
                in_specs=[in_hbm],
                out_specs=[in_vmem] * len(groups),
                scratch_shapes=[pltpu.SemaphoreType.DMA((len(places),))],
            ),
            compiler_params=params,
            name=name,
        )(r[None], parts)

    def opposite(h):
        return lax.dynamic_slice(parts, (r ^ 2, h, 0, 0, 0), (1, 1, half, rows, width))[0, 0]

    relayed_a = lax.ppermute(opposite(0), "rep", swap1)
    relayed_b = lax.ppermute(opposite(1), "rep", swap3)
    send_a, send_b, kept_a, kept_b, own = pick(
        "pick", [(1, 0)], [(3, 1)], [(3, 0)], [(1, 1)], [(0, 0), (0, 1)]
    )
    direct_a = lax.ppermute(send_a, "rep", swap1)
    direct_b = lax.ppermute(send_b, "rep", swap3)

    def relay(kept, relayed):
        return pl.pallas_call(
            relay_kernel,
            in_specs=[in_vmem] * 2,
            out_specs=in_vmem,
            out_shape=half_shape,
            compiler_params=params,
            name="relay",
        )(kept, relayed)

    second_a = lax.ppermute(relay(kept_a, relayed_a), "rep", swap3)
    second_b = lax.ppermute(relay(kept_b, relayed_b), "rep", swap1)
    presum = pl.pallas_call(
        presum_kernel,
        in_specs=[in_vmem] * 3,
        out_specs=in_vmem,
        out_shape=jax.ShapeDtypeStruct((per_row, rows, width), F32),
        compiler_params=params,
        name="presum",
    )(own, direct_a, direct_b)

    outgoing = pl.pallas_call(
        pack_kernel,
        out_shape=jax.ShapeDtypeStruct((fsdp * capacity, rows, width), BF16),
        grid_spec=pltpu.PrefetchScalarGridSpec(
            num_scalar_prefetch=1, grid=(1,), in_specs=[in_vmem] * 3, out_specs=in_vmem
        ),
        compiler_params=params,
        name="pack",
    )(slot_of, presum, second_a, second_b).reshape(fsdp, capacity, rows, width)

    arrived = lax.all_to_all(outgoing, "fsdp", split_axis=0, concat_axis=0, tiled=True)

    anywhere = pl.BlockSpec(memory_space=pl.ANY)
    factors = jax.ShapeDtypeStruct((capacity, order, order), F32)
    new_left, new_right, slot_update = pl.pallas_call(
        owner_kernel,
        in_specs=[in_vmem, in_vmem, in_vmem],
        out_specs=[anywhere, anywhere, in_vmem],
        out_shape=[factors, factors, jax.ShapeDtypeStruct((fsdp, capacity, rows, width), BF16)],
        scratch_shapes=[
            pltpu.VMEM((capacity, order, order), F32),
            pltpu.VMEM((capacity, order, order), F32),
            pltpu.SemaphoreType.DMA((2 * capacity,)),
        ],
        compiler_params=params,
        name="owner",
    )(arrived, left_factors[0, 0], right_factors[0, 0])

    returned = lax.all_to_all(slot_update, "fsdp", split_axis=0, concat_axis=0, tiled=True)

    mine_a, mine_b = pl.pallas_call(
        unpack_kernel,
        out_shape=[half_shape] * 2,
        grid_spec=pltpu.PrefetchScalarGridSpec(
            num_scalar_prefetch=1,
            grid=(1,),
            in_specs=[in_vmem],
            out_specs=[in_vmem, in_vmem],
        ),
        compiler_params=params,
        name="unpack",
    )(slot_of, returned.reshape(fsdp * capacity, rows, width))

    plus = [(i, (i + 1) % reps) for i in range(reps)]
    minus = [(i, (i - 1) % reps) for i in range(reps)]
    left_a = lax.ppermute(mine_a, "rep", plus)
    right_b = lax.ppermute(mine_b, "rep", minus)
    left_b = lax.ppermute(mine_b, "rep", plus)
    right_a = lax.ppermute(mine_a, "rep", minus)
    far_a = lax.ppermute(left_a, "rep", plus)
    far_b = lax.ppermute(right_b, "rep", minus)
    update_shape = jax.ShapeDtypeStruct((reps, 2, half, rows, width), BF16)

    def place(name, turns, halves, steps, values, before=None):
        held = [] if before is None else [before]
        size = len(steps[0])

        def where(i, t):
            turn, first = turns[-1], halves[-1]
            for k in range(len(steps) - 1):
                turn, first = jnp.where(i == k, turns[k], turn), jnp.where(i == k, halves[k], first)
            return lax.rem(t[0] + turn, reps), first, 0, 0, 0

        return pl.pallas_call(
            functools.partial(place_kernel, steps),
            out_shape=update_shape,
            grid_spec=pltpu.PrefetchScalarGridSpec(
                num_scalar_prefetch=1,
                grid=(len(steps),),
                in_specs=[in_vmem] * len(values) + [anywhere] * len(held),
                out_specs=pl.BlockSpec((1, size, half, rows, width), where),
            ),
            input_output_aliases={len(values) + 1: 0} if held else {},
            compiler_params=params,
            name=name,
        )(r[None], *values, *held)

    singles = [(0,), (1,), (2,), (3,)]
    update = place("place_first", [0, 0, 3, 1], [0, 1, 0, 1], singles, [mine_a, mine_b, left_a, right_b])
    update = place("place_second", [3, 1], [1, 0], singles[:2], [left_b, right_a], update)
    update = place("place_far", [2], [0], [(0, 1)], [far_a, far_b], update)
    return (update.reshape(reps * per_row, rows, width), new_left[None, None], new_right[None, None])


def solution(mesh):
    in_specs = (
        P("rep", None, "fsdp", None),
        P("rep", "fsdp", None, None, None),
        P("rep", "fsdp", None, None, None),
        P(),
    )
    out_specs = (
        P(None, "fsdp", None),
        P("rep", "fsdp", None, None, None),
        P("rep", "fsdp", None, None, None),
    )
    return jax.shard_map(shards, mesh=mesh, in_specs=in_specs, out_specs=out_specs, check_vma=False)
```

```python
import functools

import jax
import jax.numpy as jnp
from jax import lax
from jax.experimental import pallas as pl
from jax.experimental.pallas import tpu as pltpu
from jax.sharding import PartitionSpec as P

BF16 = jnp.bfloat16
F32 = jnp.float32
VMEM_BYTES = 36 * 1024 * 1024


def slots_of_blocks(owner_ids, capacity):
    position = jnp.arange(owner_ids.shape[0], dtype=jnp.int32)
    same_owner = owner_ids[:, None] == owner_ids[None, :]
    earlier = position[None, :] < position[:, None]
    slot_rank = jnp.sum((same_owner & earlier).astype(jnp.int32), axis=1)
    return owner_ids * capacity + slot_rank


def pick_kernel(places, table, parts, *refs):
    outs, sems = refs[:-1], refs[-1]
    copies = []
    for i, (k, first, count) in enumerate(places):
        source = parts.at[table[0] ^ k, pl.ds(first, count)]
        copies.append(pltpu.make_async_copy(source, outs[i], sems.at[i]))
    for copy in copies:
        copy.start()
    for copy in copies:
        copy.wait()


def relay_kernel(kept, relayed, *refs):
    out = refs[-1]
    out[...] = (kept[...].astype(F32) + relayed[...].astype(F32)).astype(BF16)


def presum_kernel(own, direct_a, direct_b, out):
    count = direct_a.shape[0]
    out[:count] = own[:count].astype(F32) + direct_a[...].astype(F32)
    out[count:] = own[count:].astype(F32) + direct_b[...].astype(F32)


def pack_kernel(table, presum, second_a, second_b, out):
    out[...] = jnp.zeros(out.shape, out.dtype)
    for first, second in ((0, second_a), (second_a.shape[0], second_b)):

        def move(j, carry, first=first, second=second):
            total = presum[first + j] + second[j].astype(F32)
            out[table[first + j]] = total.astype(BF16)
            return carry

        lax.fori_loop(0, second.shape[0], move, 0, unroll=4)


def dot(a, b, ca=1, cb=0):
    return lax.dot_general(a, b, (((ca,), (cb,)), ((), ())), preferred_element_type=F32)


def inverse_roots(matrices, identity):
    ys = [m * lax.rsqrt(jnp.sum(m * m) + 1e-06) for m in matrices]
    ybs = [y.astype(BF16) for y in ys]
    y2s = [dot(b, b) for b in ybs]
    ss = [2.25 * y - 1.5 * y2 + 0.25 * dot(y2.astype(BF16), b) for y, y2, b in zip(ys, y2s, ybs)]
    sbs = [s.astype(BF16) for s in ss]
    s2s = [dot(s, s) for s in sbs]
    qs = [
        -2.4375 * s + 1.6875 * s2 + dot(s2.astype(BF16), (0.0625 * s2 - 0.5625 * s).astype(BF16))
        for s, s2 in zip(ss, s2s)
    ]
    zs = [
        3.375 * identity + 1.5 * q - 1.125 * y - 0.5 * dot(b, q.astype(BF16)) for q, y, b in zip(qs, ys, ybs)
    ]
    return [z.astype(BF16) for z in zs]


def owner_kernel(arrived, left, right, new_left, new_right, out, held_left, held_right, sems):
    capacity, n = left.shape[0], left.shape[1]
    row = lax.broadcasted_iota(jnp.int32, (n, n), 0)
    col = lax.broadcasted_iota(jnp.int32, (n, n), 1)
    identity = (row == col).astype(F32)
    copies, grads, norms, factors = [], [], [], []
    for s in range(capacity):
        wide = arrived[:, s].astype(F32).reshape(n, n)
        grad = wide.astype(BF16)
        turned = grad.T
        new = (
            0.9 * left[s] + 0.1 * dot(grad, grad, 1, 1),
            0.9 * right[s] + 0.1 * dot(turned, turned, 1, 1),
        )
        for k, (held, target) in enumerate(((held_left, new_left), (held_right, new_right))):
            held[s] = new[k]
            copies.append(pltpu.make_async_copy(held.at[s], target.at[s], sems.at[2 * s + k]))
            copies[-1].start()
        grads.append(grad)
        norms.append(jnp.sum(wide * wide))
        factors.append(new)
    for s in range(capacity):
        root_left, root_right = inverse_roots(factors[s], identity)
        half = dot(root_left, grads[s]).astype(BF16)
        raw = dot(half, root_right)
        factor = jnp.sqrt(norms[s]) * lax.rsqrt(jnp.sum(raw * raw) + 1e-06)
        out[:, s] = (raw * factor).reshape(out.shape[0], out.shape[2], out.shape[3]).astype(BF16)
    for copy in copies:
        copy.wait()


def unpack_kernel(table, slots, out_a, out_b):
    half = out_a.shape[0]

    def move(j, carry):
        out_a[j] = slots[table[j]]
        out_b[j] = slots[table[half + j]]
        return carry

    lax.fori_loop(0, half, move, 0, unroll=4)


def place_kernel(steps, table, *refs):
    out = refs[-1]
    for k, step in enumerate(steps):

        @pl.when(pl.program_id(0) == k)
        def _():
            for i, part in enumerate(step):
                out[0, i] = refs[part][...]


def shards(grads, left_factors, right_factors, owners):
    reps = lax.axis_size("rep")
    fsdp = lax.axis_size("fsdp")
    r = lax.axis_index("rep").astype(jnp.int32)
    rows, width = grads.shape[2], grads.shape[3]
    capacity, order = left_factors.shape[2], left_factors.shape[3]
    per_row = grads.shape[1] // reps
    half = per_row // 2
    own_owners = lax.dynamic_index_in_dim(owners[:, :, 0], r, 0, keepdims=False)
    slot_of = slots_of_blocks(own_owners, capacity)

    swap1 = [(i, i ^ 1) for i in range(reps)]
    swap3 = [(i, i ^ 3) for i in range(reps)]
    parts = grads.reshape(reps, per_row, rows, width)
    count_a = per_row * 9 // 16
    count_b = per_row - count_a
    params = pltpu.CompilerParams(vmem_limit_bytes=VMEM_BYTES)

    in_vmem = pl.BlockSpec(memory_space=pltpu.VMEM)
    in_hbm = pl.BlockSpec(memory_space=pltpu.HBM)
    anywhere = pl.BlockSpec(memory_space=pl.ANY)

    def rows_of(count):
        return jax.ShapeDtypeStruct((count, rows, width), BF16)

    def opposite(first, count):
        return lax.dynamic_slice(parts, (r ^ 2, first, 0, 0), (1, count, rows, width))[0]

    relayed_a = lax.ppermute(opposite(0, count_a), "rep", swap1)
    relayed_b = lax.ppermute(opposite(count_a, count_b), "rep", swap3)
    places = [(1, 0, count_a), (3, count_a, count_b), (3, 0, count_a), (1, count_a, count_b), (0, 0, per_row)]
    send_a, send_b, kept_a, kept_b, own = pl.pallas_call(
        functools.partial(pick_kernel, places),
        out_shape=[rows_of(count) for _, _, count in places],
        grid_spec=pltpu.PrefetchScalarGridSpec(
            num_scalar_prefetch=1,
            grid=(1,),
            in_specs=[in_hbm],
            out_specs=[in_vmem] * len(places),
            scratch_shapes=[pltpu.SemaphoreType.DMA((len(places),))],
        ),
        compiler_params=params,
        name="pick",
    )(r[None], parts)
    direct_a = lax.ppermute(send_a, "rep", swap1)
    direct_b = lax.ppermute(send_b, "rep", swap3)

    def relay(kept, relayed, *after):
        return pl.pallas_call(
            relay_kernel,
            in_specs=[in_vmem] * 2 + [anywhere] * len(after),
            out_specs=in_vmem,
            out_shape=rows_of(kept.shape[0]),
            compiler_params=params,
            name="relay",
        )(kept, relayed, *after)

    sum_a = relay(kept_a, relayed_a)
    sum_b = relay(kept_b, relayed_b, sum_a)
    second_a = lax.ppermute(sum_a, "rep", swap3)
    second_b = lax.ppermute(sum_b, "rep", swap1)
    presum = pl.pallas_call(
        presum_kernel,
        in_specs=[in_vmem] * 3,
        out_specs=in_vmem,
        out_shape=jax.ShapeDtypeStruct((per_row, rows, width), F32),
        compiler_params=params,
        name="presum",
    )(own, direct_a, direct_b)

    outgoing = pl.pallas_call(
        pack_kernel,
        out_shape=jax.ShapeDtypeStruct((fsdp * capacity, rows, width), BF16),
        grid_spec=pltpu.PrefetchScalarGridSpec(
            num_scalar_prefetch=1, grid=(1,), in_specs=[in_vmem] * 3, out_specs=in_vmem
        ),
        compiler_params=params,
        name="pack",
    )(slot_of, presum, second_a, second_b).reshape(fsdp, capacity, rows, width)

    arrived = lax.all_to_all(outgoing, "fsdp", split_axis=0, concat_axis=0, tiled=True)

    factors = jax.ShapeDtypeStruct((capacity, order, order), F32)
    new_left, new_right, slot_update = pl.pallas_call(
        owner_kernel,
        in_specs=[in_vmem, in_vmem, in_vmem],
        out_specs=[anywhere, anywhere, in_vmem],
        out_shape=[factors, factors, jax.ShapeDtypeStruct((fsdp, capacity, rows, width), BF16)],
        scratch_shapes=[
            pltpu.VMEM((capacity, order, order), F32),
            pltpu.VMEM((capacity, order, order), F32),
            pltpu.SemaphoreType.DMA((2 * capacity,)),
        ],
        compiler_params=params,
        name="owner",
    )(arrived, left_factors[0, 0], right_factors[0, 0])

    returned = lax.all_to_all(slot_update, "fsdp", split_axis=0, concat_axis=0, tiled=True)

    mine_a, mine_b = pl.pallas_call(
        unpack_kernel,
        out_shape=[rows_of(half)] * 2,
        grid_spec=pltpu.PrefetchScalarGridSpec(
            num_scalar_prefetch=1,
            grid=(1,),
            in_specs=[in_vmem],
            out_specs=[in_vmem, in_vmem],
        ),
        compiler_params=params,
        name="unpack",
    )(slot_of, returned.reshape(fsdp * capacity, rows, width))

    plus = [(i, (i + 1) % reps) for i in range(reps)]
    minus = [(i, (i - 1) % reps) for i in range(reps)]
    left_a = lax.ppermute(mine_a, "rep", plus)
    right_b = lax.ppermute(mine_b, "rep", minus)
    left_b = lax.ppermute(mine_b, "rep", plus)
    right_a = lax.ppermute(mine_a, "rep", minus)
    far_a = lax.ppermute(left_a, "rep", plus)
    far_b = lax.ppermute(right_b, "rep", minus)
    update_shape = jax.ShapeDtypeStruct((reps, 2, half, rows, width), BF16)

    def place(name, turns, halves, steps, values, before=None):
        held = [] if before is None else [before]
        size = len(steps[0])

        def where(i, t):
            turn, first = turns[-1], halves[-1]
            for k in range(len(steps) - 1):
                turn, first = jnp.where(i == k, turns[k], turn), jnp.where(i == k, halves[k], first)
            return lax.rem(t[0] + turn, reps), first, 0, 0, 0

        return pl.pallas_call(
            functools.partial(place_kernel, steps),
            out_shape=update_shape,
            grid_spec=pltpu.PrefetchScalarGridSpec(
                num_scalar_prefetch=1,
                grid=(len(steps),),
                in_specs=[in_vmem] * len(values) + [anywhere] * len(held),
                out_specs=pl.BlockSpec((1, size, half, rows, width), where),
            ),
            input_output_aliases={len(values) + 1: 0} if held else {},
            compiler_params=params,
            name=name,
        )(r[None], *values, *held)

    singles = [(0,), (1,), (2,), (3,)]
    update = place("place_first", [0, 0, 3, 1], [0, 1, 0, 1], singles, [mine_a, mine_b, left_a, right_b])
    update = place("place_second", [3, 1], [1, 0], singles[:2], [left_b, right_a], update)
    update = place("place_far", [2], [0], [(0, 1)], [far_a, far_b], update)
    return (update.reshape(reps * per_row, rows, width), new_left[None, None], new_right[None, None])


def solution(mesh):
    in_specs = (
        P("rep", None, "fsdp", None),
        P("rep", "fsdp", None, None, None),
        P("rep", "fsdp", None, None, None),
        P(),
    )
    out_specs = (
        P(None, "fsdp", None),
        P("rep", "fsdp", None, None, None),
        P("rep", "fsdp", None, None, None),
    )
    return jax.shard_map(shards, mesh=mesh, in_specs=in_specs, out_specs=out_specs, check_vma=False)
```

```python
import functools

import jax
import jax.numpy as jnp
from jax import lax
from jax.experimental import pallas as pl
from jax.experimental.pallas import tpu as pltpu
from jax.sharding import PartitionSpec as P

BF16 = jnp.bfloat16
F32 = jnp.float32
VMEM_BYTES = 36 * 1024 * 1024


def slots_of_blocks(owner_ids, capacity):
    position = jnp.arange(owner_ids.shape[0], dtype=jnp.int32)
    same_owner = owner_ids[:, None] == owner_ids[None, :]
    earlier = position[None, :] < position[:, None]
    slot_rank = jnp.sum((same_owner & earlier).astype(jnp.int32), axis=1)
    return owner_ids * capacity + slot_rank


def pick_kernel(places, table, parts, *refs):
    outs, sems = refs[:-1], refs[-1]
    copies = []
    for i, (k, h, target, row) in enumerate(places):
        copies.append(pltpu.make_async_copy(parts.at[table[0] ^ k, h], outs[target].at[row], sems.at[i]))
    for copy in copies:
        copy.start()
    for copy in copies:
        copy.wait()


def relay_kernel(kept, relayed, out):
    out[...] = (kept[0].astype(F32) + relayed[...].astype(F32)).astype(BF16)


def presum_kernel(own, direct_a, direct_b, out):
    half = direct_a.shape[1]
    for k, direct in enumerate((direct_a, direct_b)):
        out[k * half : (k + 1) * half] = own[k].astype(F32) + direct[0].astype(F32)


def pack_kernel(table, presum, second_a, second_b, out):
    half = second_a.shape[0]
    out[...] = jnp.zeros(out.shape, out.dtype)
    for k, second in enumerate((second_a, second_b)):

        def move(j, carry, k=k, second=second):
            total = presum[k * half + j] + second[j].astype(F32)
            out[table[k * half + j]] = total.astype(BF16)
            return carry

        lax.fori_loop(0, half, move, 0, unroll=8)


def dot(a, b, ca=1, cb=0):
    return lax.dot_general(a, b, (((ca,), (cb,)), ((), ())), preferred_element_type=F32)


def inverse_roots(matrices, identity):
    ys = [m * lax.rsqrt(jnp.sum(m * m) + 1e-06) for m in matrices]
    ybs = [y.astype(BF16) for y in ys]
    y2s = [dot(b, b) for b in ybs]
    ss = [2.25 * y - 1.5 * y2 + 0.25 * dot(y2.astype(BF16), b) for y, y2, b in zip(ys, y2s, ybs)]
    sbs = [s.astype(BF16) for s in ss]
    s2s = [dot(s, s) for s in sbs]
    qs = [
        -2.4375 * s + 1.6875 * s2 + dot((0.0625 * s2 - 0.5625 * s).astype(BF16), s2.astype(BF16))
        for s, s2 in zip(ss, s2s)
    ]
    zs = [
        3.375 * identity + 1.5 * q - 1.125 * y - 0.5 * dot(q.astype(BF16), b) for q, y, b in zip(qs, ys, ybs)
    ]
    return [z.astype(BF16) for z in zs]


def owner_kernel(arrived, left, right, new_left, new_right, out, held_left, held_right, sems):
    capacity, n = left.shape[0], left.shape[1]
    row = lax.broadcasted_iota(jnp.int32, (n, n), 0)
    col = lax.broadcasted_iota(jnp.int32, (n, n), 1)
    identity = (row == col).astype(F32)
    copies, grads, norms, factors = [], [], [], []
    for s in range(capacity):
        wide = arrived[:, s].astype(F32).reshape(n, n)
        grad = wide.astype(BF16)
        turned = grad.T
        new = (
            0.9 * left[s] + 0.1 * dot(grad, grad, 1, 1),
            0.9 * right[s] + 0.1 * dot(turned, turned, 1, 1),
        )
        for k, (held, target) in enumerate(((held_left, new_left), (held_right, new_right))):
            held[s] = new[k]
            copies.append(pltpu.make_async_copy(held.at[s], target.at[s], sems.at[2 * s + k]))
            copies[-1].start()
        grads.append(grad)
        norms.append(jnp.sum(wide * wide))
        factors.append(new)
    roots = inverse_roots([m for pair in factors for m in pair], identity)
    halves = [dot(left_root, grad).astype(BF16) for left_root, grad in zip(roots[::2], grads)]
    raws = [dot(half, right_root) for half, right_root in zip(halves, roots[1::2])]
    for s, raw in enumerate(raws):
        factor = jnp.sqrt(norms[s]) * lax.rsqrt(jnp.sum(raw * raw) + 1e-06)
        out[:, s] = (raw * factor).reshape(out.shape[0], out.shape[2], out.shape[3]).astype(BF16)
    for copy in copies:
        copy.wait()


def unpack_kernel(table, slots, out_a, out_b):
    half = out_a.shape[0]

    def move(j, carry):
        out_a[j] = slots[table[j]]
        out_b[j] = slots[table[half + j]]
        return carry

    lax.fori_loop(0, half, move, 0, unroll=4)


def place_kernel(steps, table, *refs):
    out = refs[-1]
    for k, step in enumerate(steps):

        @pl.when(pl.program_id(0) == k)
        def _():
            for i, part in enumerate(step):
                out[0, i] = refs[part][...]


def shards(grads, left_factors, right_factors, owners):
    reps = lax.axis_size("rep")
    fsdp = lax.axis_size("fsdp")
    r = lax.axis_index("rep").astype(jnp.int32)
    rows, width = grads.shape[2], grads.shape[3]
    capacity, order = left_factors.shape[2], left_factors.shape[3]
    per_row = grads.shape[1] // reps
    half = per_row // 2
    own_owners = lax.dynamic_index_in_dim(owners[:, :, 0], r, 0, keepdims=False)
    slot_of = slots_of_blocks(own_owners, capacity)

    swap1 = [(i, i ^ 1) for i in range(reps)]
    swap3 = [(i, i ^ 3) for i in range(reps)]
    parts = grads.reshape(reps, 2, half, rows, width)
    params = pltpu.CompilerParams(vmem_limit_bytes=VMEM_BYTES)
    half_shape = jax.ShapeDtypeStruct((half, rows, width), BF16)

    in_vmem = pl.BlockSpec(memory_space=pltpu.VMEM)
    in_hbm = pl.BlockSpec(memory_space=pltpu.HBM)

    def pick(name, *groups):
        places = [(k, h, o, i) for o, group in enumerate(groups) for i, (k, h) in enumerate(group)]
        return pl.pallas_call(
            functools.partial(pick_kernel, places),
            out_shape=[jax.ShapeDtypeStruct((len(group), half, rows, width), BF16) for group in groups],
            grid_spec=pltpu.PrefetchScalarGridSpec(
                num_scalar_prefetch=1,
                grid=(1,),
                in_specs=[in_hbm],
                out_specs=[in_vmem] * len(groups),
                scratch_shapes=[pltpu.SemaphoreType.DMA((len(places),))],
            ),
            compiler_params=params,
            name=name,
        )(r[None], parts)

    def opposite(h):
        return lax.dynamic_slice(parts, (r ^ 2, h, 0, 0, 0), (1, 1, half, rows, width))[0, 0]

    relayed_a = lax.ppermute(opposite(0), "rep", swap1)
    relayed_b = lax.ppermute(opposite(1), "rep", swap3)
    send_a, send_b, kept_a, kept_b, own = pick(
        "pick", [(1, 0)], [(3, 1)], [(3, 0)], [(1, 1)], [(0, 0), (0, 1)]
    )
    direct_a = lax.ppermute(send_a, "rep", swap1)
    direct_b = lax.ppermute(send_b, "rep", swap3)

    def relay(kept, relayed):
        return pl.pallas_call(
            relay_kernel,
            in_specs=[in_vmem] * 2,
            out_specs=in_vmem,
            out_shape=half_shape,
            compiler_params=params,
            name="relay",
        )(kept, relayed)

    second_a = lax.ppermute(relay(kept_a, relayed_a), "rep", swap3)
    second_b = lax.ppermute(relay(kept_b, relayed_b), "rep", swap1)
    presum = pl.pallas_call(
        presum_kernel,
        in_specs=[in_vmem] * 3,
        out_specs=in_vmem,
        out_shape=jax.ShapeDtypeStruct((per_row, rows, width), F32),
        compiler_params=params,
        name="presum",
    )(own, direct_a, direct_b)

    outgoing = pl.pallas_call(
        pack_kernel,
        out_shape=jax.ShapeDtypeStruct((fsdp * capacity, rows, width), BF16),
        grid_spec=pltpu.PrefetchScalarGridSpec(
            num_scalar_prefetch=1, grid=(1,), in_specs=[in_vmem] * 3, out_specs=in_vmem
        ),
        compiler_params=params,
        name="pack",
    )(slot_of, presum, second_a, second_b).reshape(fsdp, capacity, rows, width)

    arrived = lax.all_to_all(outgoing, "fsdp", split_axis=0, concat_axis=0, tiled=True)

    anywhere = pl.BlockSpec(memory_space=pl.ANY)
    factors = jax.ShapeDtypeStruct((capacity, order, order), F32)
    new_left, new_right, slot_update = pl.pallas_call(
        owner_kernel,
        in_specs=[in_vmem, in_vmem, in_vmem],
        out_specs=[anywhere, anywhere, in_vmem],
        out_shape=[factors, factors, jax.ShapeDtypeStruct((fsdp, capacity, rows, width), BF16)],
        scratch_shapes=[
            pltpu.VMEM((capacity, order, order), F32),
            pltpu.VMEM((capacity, order, order), F32),
            pltpu.SemaphoreType.DMA((2 * capacity,)),
        ],
        compiler_params=params,
        name="owner",
    )(arrived, left_factors[0, 0], right_factors[0, 0])

    returned = lax.all_to_all(slot_update, "fsdp", split_axis=0, concat_axis=0, tiled=True)

    mine_a, mine_b = pl.pallas_call(
        unpack_kernel,
        out_shape=[half_shape] * 2,
        grid_spec=pltpu.PrefetchScalarGridSpec(
            num_scalar_prefetch=1,
            grid=(1,),
            in_specs=[in_vmem],
            out_specs=[in_vmem, in_vmem],
        ),
        compiler_params=params,
        name="unpack",
    )(slot_of, returned.reshape(fsdp * capacity, rows, width))

    plus = [(i, (i + 1) % reps) for i in range(reps)]
    minus = [(i, (i - 1) % reps) for i in range(reps)]
    left_a = lax.ppermute(mine_a, "rep", plus)
    right_b = lax.ppermute(mine_b, "rep", minus)
    left_b = lax.ppermute(mine_b, "rep", plus)
    right_a = lax.ppermute(mine_a, "rep", minus)
    far_a = lax.ppermute(left_a, "rep", plus)
    far_b = lax.ppermute(right_b, "rep", minus)
    update_shape = jax.ShapeDtypeStruct((reps, 2, half, rows, width), BF16)

    def place(name, turns, halves, steps, values, before=None):
        held = [] if before is None else [before]
        size = len(steps[0])

        def where(i, t):
            turn, first = turns[-1], halves[-1]
            for k in range(len(steps) - 1):
                turn, first = jnp.where(i == k, turns[k], turn), jnp.where(i == k, halves[k], first)
            return lax.rem(t[0] + turn, reps), first, 0, 0, 0

        return pl.pallas_call(
            functools.partial(place_kernel, steps),
            out_shape=update_shape,
            grid_spec=pltpu.PrefetchScalarGridSpec(
                num_scalar_prefetch=1,
                grid=(len(steps),),
                in_specs=[in_vmem] * len(values) + [anywhere] * len(held),
                out_specs=pl.BlockSpec((1, size, half, rows, width), where),
            ),
            input_output_aliases={len(values) + 1: 0} if held else {},
            compiler_params=params,
            name=name,
        )(r[None], *values, *held)

    singles = [(0,), (1,), (2,), (3,)]
    update = place("place_first", [0, 0, 3, 1], [0, 1, 0, 1], singles, [mine_a, mine_b, left_a, right_b])
    update = place("place_second", [3, 1], [1, 0], singles[:2], [left_b, right_a], update)
    update = place("place_far", [2], [0], [(0, 1)], [far_a, far_b], update)
    return (update.reshape(reps * per_row, rows, width), new_left[None, None], new_right[None, None])


def solution(mesh):
    in_specs = (
        P("rep", None, "fsdp", None),
        P("rep", "fsdp", None, None, None),
        P("rep", "fsdp", None, None, None),
        P(),
    )
    out_specs = (
        P(None, "fsdp", None),
        P("rep", "fsdp", None, None, None),
        P("rep", "fsdp", None, None, None),
    )
    return jax.shard_map(shards, mesh=mesh, in_specs=in_specs, out_specs=out_specs, check_vma=False)
```

```python
import functools

import jax
import jax.numpy as jnp
from jax import lax
from jax.experimental import pallas as pl
from jax.experimental.pallas import tpu as pltpu
from jax.sharding import PartitionSpec as P

BF16 = jnp.bfloat16
F32 = jnp.float32
VMEM_BYTES = 36 * 1024 * 1024


def slots_of_blocks(owner_ids, capacity):
    position = jnp.arange(owner_ids.shape[0], dtype=jnp.int32)
    same_owner = owner_ids[:, None] == owner_ids[None, :]
    earlier = position[None, :] < position[:, None]
    slot_rank = jnp.sum((same_owner & earlier).astype(jnp.int32), axis=1)
    return owner_ids * capacity + slot_rank


def pick_kernel(places, table, parts, *refs):
    outs, sems = refs[:-1], refs[-1]
    copies = []
    for i, (k, h, target, row) in enumerate(places):
        copies.append(pltpu.make_async_copy(parts.at[table[0] ^ k, h], outs[target].at[row], sems.at[i]))
    for copy in copies:
        copy.start()
    for copy in copies:
        copy.wait()


def relay_kernel(kept, relayed, out):
    out[...] = (kept[0].astype(F32) + relayed[...].astype(F32)).astype(BF16)


def presum_kernel(own, direct_a, direct_b, out):
    half = direct_a.shape[1]
    for k, direct in enumerate((direct_a, direct_b)):
        out[k * half : (k + 1) * half] = own[k].astype(F32) + direct[0].astype(F32)


def pack_kernel(table, presum, second_a, second_b, out):
    half = second_a.shape[0]
    out[...] = jnp.zeros(out.shape, out.dtype)
    for k, second in enumerate((second_a, second_b)):

        def move(j, carry, k=k, second=second):
            total = presum[k * half + j] + second[j].astype(F32)
            out[table[k * half + j]] = total.astype(BF16)
            return carry

        lax.fori_loop(0, half, move, 0, unroll=8)


def dot(a, b, ca=1, cb=0):
    return lax.dot_general(a, b, (((ca,), (cb,)), ((), ())), preferred_element_type=F32)


def inverse_roots(matrices, identity):
    scales = [lax.rsqrt(jnp.sum(m * m) + 1e-06) for m in matrices]
    ybs = [(m * c).astype(BF16) for m, c in zip(matrices, scales)]
    y2s = [dot(b, b) for b in ybs]
    ss = [
        (2.25 * c) * m - 1.5 * y2 + 0.25 * dot(y2.astype(BF16), b)
        for m, c, y2, b in zip(matrices, scales, y2s, ybs)
    ]
    sbs = [s.astype(BF16) for s in ss]
    s2s = [dot(s, s) for s in sbs]
    qs = [
        -2.4375 * s + 1.6875 * s2 + dot((0.0625 * s2 - 0.5625 * s).astype(BF16), s2.astype(BF16))
        for s, s2 in zip(ss, s2s)
    ]
    zs = [
        3.375 * identity + 1.5 * q - (1.125 * c) * m - 0.5 * dot(q.astype(BF16), b)
        for q, m, c, b in zip(qs, matrices, scales, ybs)
    ]
    return [z.astype(BF16) for z in zs]


def owner_kernel(arrived, left, right, new_left, new_right, out, held_left, held_right, sems):
    capacity, n = left.shape[0], left.shape[1]
    row = lax.broadcasted_iota(jnp.int32, (n, n), 0)
    col = lax.broadcasted_iota(jnp.int32, (n, n), 1)
    identity = (row == col).astype(F32)
    wides = [arrived[:, s].astype(F32).reshape(n, n) for s in range(capacity)]
    grads = [wide.astype(BF16) for wide in wides]
    norms = [jnp.sum(wide * wide) for wide in wides]
    turned = [grad.T for grad in grads]
    grams = [dot(g, g, 1, 1) for pair in zip(grads, turned) for g in pair]
    factors = [0.9 * (left, right)[k % 2][k // 2] + 0.1 * gram for k, gram in enumerate(grams)]
    copies = []
    for k, factor in enumerate(factors):
        held, target = ((held_left, new_left), (held_right, new_right))[k % 2]
        held[k // 2] = factor
        copies.append(pltpu.make_async_copy(held.at[k // 2], target.at[k // 2], sems.at[k]))
        copies[-1].start()
    roots = inverse_roots(factors, identity)
    halves = [dot(root_left, grad).astype(BF16) for root_left, grad in zip(roots[::2], grads)]
    raws = [dot(half, root_right) for half, root_right in zip(halves, roots[1::2])]
    for s, raw in enumerate(raws):
        scale = jnp.sqrt(norms[s]) * lax.rsqrt(jnp.sum(raw * raw) + 1e-06)
        out[:, s] = (raw * scale).reshape(out.shape[0], out.shape[2], out.shape[3]).astype(BF16)
    for copy in copies:
        copy.wait()


def unpack_kernel(table, slots, out_a, out_b):
    half = out_a.shape[0]

    def move(j, carry):
        out_a[j] = slots[table[j]]
        out_b[j] = slots[table[half + j]]
        return carry

    lax.fori_loop(0, half, move, 0, unroll=4)


def place_kernel(steps, table, *refs):
    out = refs[-1]
    for k, step in enumerate(steps):

        @pl.when(pl.program_id(0) == k)
        def _():
            for i, part in enumerate(step):
                out[0, i] = refs[part][...]


def shards(grads, left_factors, right_factors, owners):
    reps = lax.axis_size("rep")
    fsdp = lax.axis_size("fsdp")
    r = lax.axis_index("rep").astype(jnp.int32)
    rows, width = grads.shape[2], grads.shape[3]
    capacity, order = left_factors.shape[2], left_factors.shape[3]
    per_row = grads.shape[1] // reps
    half = per_row // 2
    own_owners = lax.dynamic_index_in_dim(owners[:, :, 0], r, 0, keepdims=False)
    slot_of = slots_of_blocks(own_owners, capacity)

    swap1 = [(i, i ^ 1) for i in range(reps)]
    swap3 = [(i, i ^ 3) for i in range(reps)]
    parts = grads.reshape(reps, 2, half, rows, width)
    params = pltpu.CompilerParams(vmem_limit_bytes=VMEM_BYTES)
    half_shape = jax.ShapeDtypeStruct((half, rows, width), BF16)

    in_vmem = pl.BlockSpec(memory_space=pltpu.VMEM)
    in_hbm = pl.BlockSpec(memory_space=pltpu.HBM)

    def pick(name, *groups):
        places = [(k, h, o, i) for o, group in enumerate(groups) for i, (k, h) in enumerate(group)]
        return pl.pallas_call(
            functools.partial(pick_kernel, places),
            out_shape=[jax.ShapeDtypeStruct((len(group), half, rows, width), BF16) for group in groups],
            grid_spec=pltpu.PrefetchScalarGridSpec(
                num_scalar_prefetch=1,
                grid=(1,),
                in_specs=[in_hbm],
                out_specs=[in_vmem] * len(groups),
                scratch_shapes=[pltpu.SemaphoreType.DMA((len(places),))],
            ),
            compiler_params=params,
            name=name,
        )(r[None], parts)

    def opposite(h):
        return lax.dynamic_slice(parts, (r ^ 2, h, 0, 0, 0), (1, 1, half, rows, width))[0, 0]

    relayed_a = lax.ppermute(opposite(0), "rep", swap1)
    relayed_b = lax.ppermute(opposite(1), "rep", swap3)
    send_a, send_b, kept_a, kept_b, own = pick(
        "pick", [(1, 0)], [(3, 1)], [(3, 0)], [(1, 1)], [(0, 0), (0, 1)]
    )
    direct_a = lax.ppermute(send_a, "rep", swap1)
    direct_b = lax.ppermute(send_b, "rep", swap3)

    def relay(kept, relayed):
        return pl.pallas_call(
            relay_kernel,
            in_specs=[in_vmem] * 2,
            out_specs=in_vmem,
            out_shape=half_shape,
            compiler_params=params,
            name="relay",
        )(kept, relayed)

    second_a = lax.ppermute(relay(kept_a, relayed_a), "rep", swap3)
    second_b = lax.ppermute(relay(kept_b, relayed_b), "rep", swap1)
    presum = pl.pallas_call(
        presum_kernel,
        in_specs=[in_vmem] * 3,
        out_specs=in_vmem,
        out_shape=jax.ShapeDtypeStruct((per_row, rows, width), F32),
        compiler_params=params,
        name="presum",
    )(own, direct_a, direct_b)

    outgoing = pl.pallas_call(
        pack_kernel,
        out_shape=jax.ShapeDtypeStruct((fsdp * capacity, rows, width), BF16),
        grid_spec=pltpu.PrefetchScalarGridSpec(
            num_scalar_prefetch=1, grid=(1,), in_specs=[in_vmem] * 3, out_specs=in_vmem
        ),
        compiler_params=params,
        name="pack",
    )(slot_of, presum, second_a, second_b).reshape(fsdp, capacity, rows, width)

    arrived = lax.all_to_all(outgoing, "fsdp", split_axis=0, concat_axis=0, tiled=True)

    anywhere = pl.BlockSpec(memory_space=pl.ANY)
    factors = jax.ShapeDtypeStruct((capacity, order, order), F32)
    new_left, new_right, slot_update = pl.pallas_call(
        owner_kernel,
        in_specs=[in_vmem, in_vmem, in_vmem],
        out_specs=[anywhere, anywhere, in_vmem],
        out_shape=[factors, factors, jax.ShapeDtypeStruct((fsdp, capacity, rows, width), BF16)],
        scratch_shapes=[
            pltpu.VMEM((capacity, order, order), F32),
            pltpu.VMEM((capacity, order, order), F32),
            pltpu.SemaphoreType.DMA((2 * capacity,)),
        ],
        compiler_params=params,
        name="owner",
    )(arrived, left_factors[0, 0], right_factors[0, 0])

    returned = lax.all_to_all(slot_update, "fsdp", split_axis=0, concat_axis=0, tiled=True)

    mine_a, mine_b = pl.pallas_call(
        unpack_kernel,
        out_shape=[half_shape] * 2,
        grid_spec=pltpu.PrefetchScalarGridSpec(
            num_scalar_prefetch=1,
            grid=(1,),
            in_specs=[in_vmem],
            out_specs=[in_vmem, in_vmem],
        ),
        compiler_params=params,
        name="unpack",
    )(slot_of, returned.reshape(fsdp * capacity, rows, width))

    plus = [(i, (i + 1) % reps) for i in range(reps)]
    minus = [(i, (i - 1) % reps) for i in range(reps)]
    left_a = lax.ppermute(mine_a, "rep", plus)
    right_b = lax.ppermute(mine_b, "rep", minus)
    left_b = lax.ppermute(mine_b, "rep", plus)
    right_a = lax.ppermute(mine_a, "rep", minus)
    far_a = lax.ppermute(left_a, "rep", plus)
    far_b = lax.ppermute(right_b, "rep", minus)
    update_shape = jax.ShapeDtypeStruct((reps, 2, half, rows, width), BF16)

    def place(name, turns, halves, steps, values, before=None):
        held = [] if before is None else [before]
        size = len(steps[0])

        def where(i, t):
            turn, first = turns[-1], halves[-1]
            for k in range(len(steps) - 1):
                turn, first = jnp.where(i == k, turns[k], turn), jnp.where(i == k, halves[k], first)
            return lax.rem(t[0] + turn, reps), first, 0, 0, 0

        return pl.pallas_call(
            functools.partial(place_kernel, steps),
            out_shape=update_shape,
            grid_spec=pltpu.PrefetchScalarGridSpec(
                num_scalar_prefetch=1,
                grid=(len(steps),),
                in_specs=[in_vmem] * len(values) + [anywhere] * len(held),
                out_specs=pl.BlockSpec((1, size, half, rows, width), where),
            ),
            input_output_aliases={len(values) + 1: 0} if held else {},
            compiler_params=params,
            name=name,
        )(r[None], *values, *held)

    singles = [(0,), (1,), (2,), (3,)]
    update = place("place_first", [0, 0, 3, 1], [0, 1, 0, 1], singles, [mine_a, mine_b, left_a, right_b])
    update = place("place_second", [3, 1], [1, 0], singles[:2], [left_b, right_a], update)
    update = place("place_far", [2], [0], [(0, 1)], [far_a, far_b], update)
    return (update.reshape(reps * per_row, rows, width), new_left[None, None], new_right[None, None])


def solution(mesh):
    in_specs = (
        P("rep", None, "fsdp", None),
        P("rep", "fsdp", None, None, None),
        P("rep", "fsdp", None, None, None),
        P(),
    )
    out_specs = (
        P(None, "fsdp", None),
        P("rep", "fsdp", None, None, None),
        P("rep", "fsdp", None, None, None),
    )
    return jax.shard_map(shards, mesh=mesh, in_specs=in_specs, out_specs=out_specs, check_vma=False)
```

```python
import functools

import jax
import jax.numpy as jnp
from jax import lax
from jax.experimental import pallas as pl
from jax.experimental.pallas import tpu as pltpu
from jax.sharding import PartitionSpec as P

BF16 = jnp.bfloat16
F32 = jnp.float32
VMEM_BYTES = 36 * 1024 * 1024


def slots_of_blocks(owner_ids, capacity):
    position = jnp.arange(owner_ids.shape[0], dtype=jnp.int32)
    same_owner = owner_ids[:, None] == owner_ids[None, :]
    earlier = position[None, :] < position[:, None]
    slot_rank = jnp.sum((same_owner & earlier).astype(jnp.int32), axis=1)
    return owner_ids * capacity + slot_rank


def pick_kernel(places, table, parts, *refs):
    outs, sems = refs[:-1], refs[-1]
    copies = []
    for i, (k, h, target, row) in enumerate(places):
        copies.append(pltpu.make_async_copy(parts.at[table[0] ^ k, h], outs[target].at[row], sems.at[i]))
    for copy in copies:
        copy.start()
    for copy in copies:
        copy.wait()


def relay_kernel(kept, relayed, out):
    out[...] = (kept[0].astype(F32) + relayed[...].astype(F32)).astype(BF16)


def presum_kernel(own, direct_a, direct_b, out):
    half = direct_a.shape[1]
    for k, direct in enumerate((direct_a, direct_b)):
        out[k * half : (k + 1) * half] = own[k].astype(F32) + direct[0].astype(F32)


def pack_kernel(table, presum, second_a, second_b, out):
    half = second_a.shape[0]
    out[...] = jnp.zeros(out.shape, out.dtype)
    for k, second in enumerate((second_a, second_b)):

        def move(j, carry, k=k, second=second):
            total = presum[k * half + j] + second[j].astype(F32)
            out[table[k * half + j]] = total.astype(BF16)
            return carry

        lax.fori_loop(0, half, move, 0, unroll=8)


def dot(a, b, ca=1, cb=0):
    return lax.dot_general(a, b, (((ca,), (cb,)), ((), ())), preferred_element_type=F32)


def inverse_roots(matrices, identity):
    scales = [lax.rsqrt(jnp.sum(m * m) + 1e-06) for m in matrices]
    ybs = [(m * c).astype(BF16) for m, c in zip(matrices, scales)]
    y2s = [dot(b, b) for b in ybs]
    ss = [
        (2.25 * c) * m - 1.5 * y2 + 0.25 * dot(y2.astype(BF16), b)
        for m, c, y2, b in zip(matrices, scales, y2s, ybs)
    ]
    sbs = [s.astype(BF16) for s in ss]
    s2s = [dot(s, s) for s in sbs]
    qs = [
        -2.4375 * s + 1.6875 * s2 + dot((0.0625 * s2 - 0.5625 * s).astype(BF16), s2.astype(BF16))
        for s, s2 in zip(ss, s2s)
    ]
    zs = [
        3.375 * identity + 1.5 * q - (1.125 * c) * m - 0.5 * dot(q.astype(BF16), b)
        for q, m, c, b in zip(qs, matrices, scales, ybs)
    ]
    return [z.astype(BF16) for z in zs]


def owner_kernel(arrived, left, right, new_left, new_right, out, held_left, held_right, sems):
    capacity, n = left.shape[0], left.shape[1]
    row = lax.broadcasted_iota(jnp.int32, (n, n), 0)
    col = lax.broadcasted_iota(jnp.int32, (n, n), 1)
    identity = (row == col).astype(F32)
    wides = [arrived[:, s].astype(F32).reshape(n, n) for s in range(capacity)]
    grads = [wide.astype(BF16) for wide in wides]
    norms = [jnp.sum(wide * wide) for wide in wides]
    turned = [grad.T for grad in grads]
    grams = [dot(g, g, 1, 1) for pair in zip(grads, turned) for g in pair]
    factors = [0.9 * (left, right)[k % 2][k // 2] + 0.1 * gram for k, gram in enumerate(grams)]
    copies = []
    for k, factor in enumerate(factors):
        held, target = ((held_left, new_left), (held_right, new_right))[k % 2]
        held[k // 2] = factor
        copies.append(pltpu.make_async_copy(held.at[k // 2], target.at[k // 2], sems.at[k]))
        copies[-1].start()
    roots = inverse_roots(factors, identity)
    halves = [dot(root_left, grad).astype(BF16) for root_left, grad in zip(roots[::2], grads)]
    raws = [dot(half, root_right) for half, root_right in zip(halves, roots[1::2])]
    for s, raw in enumerate(raws):
        scale = jnp.sqrt(norms[s]) * lax.rsqrt(jnp.sum(raw * raw) + 1e-06)
        out[:, s] = (raw * scale).reshape(out.shape[0], out.shape[2], out.shape[3]).astype(BF16)
    for copy in copies:
        copy.wait()


def unpack_kernel(table, slots, out_a, out_b):
    half = out_a.shape[0]

    def move(j, carry):
        out_a[j] = slots[table[j]]
        out_b[j] = slots[table[half + j]]
        return carry

    lax.fori_loop(0, half, move, 0, unroll=4)


def place_kernel(steps, table, *refs):
    out = refs[-1]
    for k, step in enumerate(steps):

        @pl.when(pl.program_id(0) == k)
        def _():
            for i, part in enumerate(step):
                out[0, i] = refs[part][...]


def shards(grads, left_factors, right_factors, owners):
    reps = lax.axis_size("rep")
    fsdp = lax.axis_size("fsdp")
    r = lax.axis_index("rep").astype(jnp.int32)
    rows, width = grads.shape[2], grads.shape[3]
    capacity, order = left_factors.shape[2], left_factors.shape[3]
    per_row = grads.shape[1] // reps
    half = per_row // 2
    own_owners = lax.dynamic_index_in_dim(owners[:, :, 0], r, 0, keepdims=False)
    slot_of = slots_of_blocks(own_owners, capacity)

    swap1 = [(i, i ^ 1) for i in range(reps)]
    swap3 = [(i, i ^ 3) for i in range(reps)]
    parts = grads.reshape(reps, 2, half, rows, width)
    params = pltpu.CompilerParams(vmem_limit_bytes=VMEM_BYTES)
    half_shape = jax.ShapeDtypeStruct((half, rows, width), BF16)

    in_vmem = pl.BlockSpec(memory_space=pltpu.VMEM)
    in_hbm = pl.BlockSpec(memory_space=pltpu.HBM)

    def pick(name, *groups):
        places = [(k, h, o, i) for o, group in enumerate(groups) for i, (k, h) in enumerate(group)]
        return pl.pallas_call(
            functools.partial(pick_kernel, places),
            out_shape=[jax.ShapeDtypeStruct((len(group), half, rows, width), BF16) for group in groups],
            grid_spec=pltpu.PrefetchScalarGridSpec(
                num_scalar_prefetch=1,
                grid=(1,),
                in_specs=[in_hbm],
                out_specs=[in_vmem] * len(groups),
                scratch_shapes=[pltpu.SemaphoreType.DMA((len(places),))],
            ),
            compiler_params=params,
            name=name,
        )(r[None], parts)

    def opposite(h):
        return lax.dynamic_slice(parts, (r ^ 2, h, 0, 0, 0), (1, 1, half, rows, width))[0, 0]

    relayed_a = lax.ppermute(opposite(0), "rep", swap1)
    relayed_b = lax.ppermute(opposite(1), "rep", swap3)
    send_a, send_b, kept_a, kept_b, own = pick(
        "pick", [(1, 0)], [(3, 1)], [(3, 0)], [(1, 1)], [(0, 0), (0, 1)]
    )
    direct_a = lax.ppermute(send_a, "rep", swap1)
    direct_b = lax.ppermute(send_b, "rep", swap3)

    def relay(kept, relayed):
        return pl.pallas_call(
            relay_kernel,
            in_specs=[in_vmem] * 2,
            out_specs=in_vmem,
            out_shape=half_shape,
            compiler_params=params,
            name="relay",
        )(kept, relayed)

    second_a = lax.ppermute(relay(kept_a, relayed_a), "rep", swap3)
    second_b = lax.ppermute(relay(kept_b, relayed_b), "rep", swap1)
    presum = pl.pallas_call(
        presum_kernel,
        in_specs=[in_vmem] * 3,
        out_specs=in_vmem,
        out_shape=jax.ShapeDtypeStruct((per_row, rows, width), F32),
        compiler_params=params,
        name="presum",
    )(own, direct_a, direct_b)

    outgoing = pl.pallas_call(
        pack_kernel,
        out_shape=jax.ShapeDtypeStruct((fsdp * capacity, rows, width), BF16),
        grid_spec=pltpu.PrefetchScalarGridSpec(
            num_scalar_prefetch=1, grid=(1,), in_specs=[in_vmem] * 3, out_specs=in_vmem
        ),
        compiler_params=params,
        name="pack",
    )(slot_of, presum, second_a, second_b).reshape(fsdp, capacity, rows, width)

    arrived = lax.all_to_all(outgoing, "fsdp", split_axis=0, concat_axis=0, tiled=True)

    anywhere = pl.BlockSpec(memory_space=pl.ANY)
    factors = jax.ShapeDtypeStruct((capacity, order, order), F32)
    new_left, new_right, slot_update = pl.pallas_call(
        owner_kernel,
        in_specs=[in_vmem, in_vmem, in_vmem],
        out_specs=[anywhere, anywhere, in_vmem],
        out_shape=[factors, factors, jax.ShapeDtypeStruct((fsdp, capacity, rows, width), BF16)],
        scratch_shapes=[
            pltpu.VMEM((capacity, order, order), F32),
            pltpu.VMEM((capacity, order, order), F32),
            pltpu.SemaphoreType.DMA((2 * capacity,)),
        ],
        compiler_params=params,
        name="owner",
    )(arrived, left_factors[0, 0], right_factors[0, 0])

    returned = lax.all_to_all(slot_update, "fsdp", split_axis=0, concat_axis=0, tiled=True)

    mine_a, mine_b = pl.pallas_call(
        unpack_kernel,
        out_shape=[half_shape] * 2,
        grid_spec=pltpu.PrefetchScalarGridSpec(
            num_scalar_prefetch=1,
            grid=(1,),
            in_specs=[in_vmem],
            out_specs=[in_vmem, in_vmem],
        ),
        compiler_params=params,
        name="unpack",
    )(slot_of, returned.reshape(fsdp * capacity, rows, width))

    near1_a = lax.ppermute(mine_a, "rep", swap1)
    near3_b = lax.ppermute(mine_b, "rep", swap3)
    near1_b = lax.ppermute(mine_b, "rep", swap1)
    near3_a = lax.ppermute(mine_a, "rep", swap3)
    far_b = lax.ppermute(near3_b, "rep", swap1)
    far_a = lax.ppermute(near1_a, "rep", swap3)
    update_shape = jax.ShapeDtypeStruct((reps, 2, half, rows, width), BF16)

    def place(name, turns, halves, steps, values, before=None):
        held = [] if before is None else [before]
        size = len(steps[0])

        def where(i, t):
            turn, first = turns[-1], halves[-1]
            for k in range(len(steps) - 1):
                turn, first = jnp.where(i == k, turns[k], turn), jnp.where(i == k, halves[k], first)
            return t[0] ^ turn, first, 0, 0, 0

        return pl.pallas_call(
            functools.partial(place_kernel, steps),
            out_shape=update_shape,
            grid_spec=pltpu.PrefetchScalarGridSpec(
                num_scalar_prefetch=1,
                grid=(len(steps),),
                in_specs=[in_vmem] * len(values) + [anywhere] * len(held),
                out_specs=pl.BlockSpec((1, size, half, rows, width), where),
            ),
            input_output_aliases={len(values) + 1: 0} if held else {},
            compiler_params=params,
            name=name,
        )(r[None], *values, *held)

    singles = [(0,), (1,), (2,), (3,)]
    update = place("place_first", [0, 0, 1, 3], [0, 1, 0, 1], singles, [mine_a, mine_b, near1_a, near3_b])
    update = place("place_second", [1, 3], [1, 0], singles[:2], [near1_b, near3_a], update)
    update = place("place_far", [2], [0], [(0, 1)], [far_a, far_b], update)
    return (update.reshape(reps * per_row, rows, width), new_left[None, None], new_right[None, None])


def solution(mesh):
    in_specs = (
        P("rep", None, "fsdp", None),
        P("rep", "fsdp", None, None, None),
        P("rep", "fsdp", None, None, None),
        P(),
    )
    out_specs = (
        P(None, "fsdp", None),
        P("rep", "fsdp", None, None, None),
        P("rep", "fsdp", None, None, None),
    )
    return jax.shard_map(shards, mesh=mesh, in_specs=in_specs, out_specs=out_specs, check_vma=False)
```

```python
import functools

import jax
import jax.numpy as jnp
from jax import lax
from jax.experimental import pallas as pl
from jax.experimental.pallas import tpu as pltpu
from jax.sharding import PartitionSpec as P

BF16 = jnp.bfloat16
F32 = jnp.float32
VMEM_BYTES = 36 * 1024 * 1024


def slots_of_blocks(owner_ids, capacity):
    position = jnp.arange(owner_ids.shape[0], dtype=jnp.int32)
    same_owner = owner_ids[:, None] == owner_ids[None, :]
    earlier = position[None, :] < position[:, None]
    slot_rank = jnp.sum((same_owner & earlier).astype(jnp.int32), axis=1)
    return owner_ids * capacity + slot_rank


def pick_kernel(places, table, parts, *refs):
    outs, sems = refs[:-1], refs[-1]
    copies = []
    for i, (k, h, target, row) in enumerate(places):
        copies.append(pltpu.make_async_copy(parts.at[table[0] ^ k, h], outs[target].at[row], sems.at[i]))
    for copy in copies:
        copy.start()
    for copy in copies:
        copy.wait()


def relay_kernel(kept, relayed, out):
    out[...] = (kept[0].astype(F32) + relayed[...].astype(F32)).astype(BF16)


def presum_kernel(own, direct_a, direct_b, out):
    half = direct_a.shape[1]
    for k, direct in enumerate((direct_a, direct_b)):
        out[k * half : (k + 1) * half] = own[k].astype(F32) + direct[0].astype(F32)


def pack_kernel(table, presum, second_a, second_b, out, held, slots, sem):
    half = second_a.shape[0]
    fetch = pltpu.make_async_copy(table, slots, sem)
    fetch.start()
    out[...] = jnp.zeros(out.shape, out.dtype)
    held[:half] = (presum[:half] + second_a[...].astype(F32)).astype(BF16)
    held[half:] = (presum[half:] + second_b[...].astype(F32)).astype(BF16)
    fetch.wait()

    def move(j, carry):
        out[slots[j]] = held[j]
        return carry

    lax.fori_loop(0, 2 * half, move, 0, unroll=8)


def dot(a, b, ca=1, cb=0):
    return lax.dot_general(a, b, (((ca,), (cb,)), ((), ())), preferred_element_type=F32)


def inverse_roots(matrices, identity):
    scales = [lax.rsqrt(jnp.sum(m * m) + 1e-06) for m in matrices]
    ybs = [(m * c).astype(BF16) for m, c in zip(matrices, scales)]
    y2s = [dot(b, b) for b in ybs]
    ss = [
        (2.25 * c) * m - 1.5 * y2 + 0.25 * dot(y2.astype(BF16), b)
        for m, c, y2, b in zip(matrices, scales, y2s, ybs)
    ]
    sbs = [s.astype(BF16) for s in ss]
    s2s = [dot(s, s) for s in sbs]
    qs = [
        -2.4375 * s + 1.6875 * s2 + dot((0.0625 * s2 - 0.5625 * s).astype(BF16), s2.astype(BF16))
        for s, s2 in zip(ss, s2s)
    ]
    zs = [
        3.375 * identity + 1.5 * q - (1.125 * c) * m - 0.5 * dot(q.astype(BF16), b)
        for q, m, c, b in zip(qs, matrices, scales, ybs)
    ]
    return [z.astype(BF16) for z in zs]


def owner_kernel(arrived, left, right, new_left, new_right, out, held_left, held_right, sems):
    capacity, n = left.shape[0], left.shape[1]
    row = lax.broadcasted_iota(jnp.int32, (n, n), 0)
    col = lax.broadcasted_iota(jnp.int32, (n, n), 1)
    identity = (row == col).astype(F32)
    wides = [arrived[:, s].astype(F32).reshape(n, n) for s in range(capacity)]
    grads = [wide.astype(BF16) for wide in wides]
    norms = [jnp.sum(wide * wide) for wide in wides]
    turned = [grad.T for grad in grads]
    grams = [dot(g, g, 1, 1) for pair in zip(grads, turned) for g in pair]
    factors = [0.9 * (left, right)[k % 2][k // 2] + 0.1 * gram for k, gram in enumerate(grams)]
    copies = []
    for k, factor in enumerate(factors):
        held, target = ((held_left, new_left), (held_right, new_right))[k % 2]
        held[k // 2] = factor
        copies.append(pltpu.make_async_copy(held.at[k // 2], target.at[k // 2], sems.at[k]))
        copies[-1].start()
    roots = inverse_roots(factors, identity)
    halves = [dot(root_left, grad).astype(BF16) for root_left, grad in zip(roots[::2], grads)]
    raws = [dot(half, root_right) for half, root_right in zip(halves, roots[1::2])]
    for s, raw in enumerate(raws):
        scale = jnp.sqrt(norms[s]) * lax.rsqrt(jnp.sum(raw * raw) + 1e-06)
        out[:, s] = (raw * scale).reshape(out.shape[0], out.shape[2], out.shape[3]).astype(BF16)
    for copy in copies:
        copy.wait()


def unpack_kernel(table, slots, out_a, out_b):
    half = out_a.shape[0]

    def move(j, carry):
        out_a[j] = slots[table[j]]
        out_b[j] = slots[table[half + j]]
        return carry

    lax.fori_loop(0, half, move, 0, unroll=4)


def place_kernel(steps, table, *refs):
    out = refs[-1]
    for k, step in enumerate(steps):

        @pl.when(pl.program_id(0) == k)
        def _():
            for i, part in enumerate(step):
                out[0, i] = refs[part][...]


def shards(grads, left_factors, right_factors, owners):
    reps = lax.axis_size("rep")
    fsdp = lax.axis_size("fsdp")
    r = lax.axis_index("rep").astype(jnp.int32)
    rows, width = grads.shape[2], grads.shape[3]
    capacity, order = left_factors.shape[2], left_factors.shape[3]
    per_row = grads.shape[1] // reps
    half = per_row // 2
    own_owners = lax.dynamic_index_in_dim(owners[:, :, 0], r, 0, keepdims=False)
    slot_of = slots_of_blocks(own_owners, capacity)

    swap1 = [(i, i ^ 1) for i in range(reps)]
    swap3 = [(i, i ^ 3) for i in range(reps)]
    parts = grads.reshape(reps, 2, half, rows, width)
    params = pltpu.CompilerParams(vmem_limit_bytes=VMEM_BYTES)
    half_shape = jax.ShapeDtypeStruct((half, rows, width), BF16)

    in_vmem = pl.BlockSpec(memory_space=pltpu.VMEM)
    in_hbm = pl.BlockSpec(memory_space=pltpu.HBM)

    def pick(name, *groups):
        places = [(k, h, o, i) for o, group in enumerate(groups) for i, (k, h) in enumerate(group)]
        return pl.pallas_call(
            functools.partial(pick_kernel, places),
            out_shape=[jax.ShapeDtypeStruct((len(group), half, rows, width), BF16) for group in groups],
            grid_spec=pltpu.PrefetchScalarGridSpec(
                num_scalar_prefetch=1,
                grid=(1,),
                in_specs=[in_hbm],
                out_specs=[in_vmem] * len(groups),
                scratch_shapes=[pltpu.SemaphoreType.DMA((len(places),))],
            ),
            compiler_params=params,
            name=name,
        )(r[None], parts)

    def opposite(h):
        return lax.dynamic_slice(parts, (r ^ 2, h, 0, 0, 0), (1, 1, half, rows, width))[0, 0]

    relayed_a = lax.ppermute(opposite(0), "rep", swap1)
    relayed_b = lax.ppermute(opposite(1), "rep", swap3)
    send_a, send_b, kept_a, kept_b, own = pick(
        "pick", [(1, 0)], [(3, 1)], [(3, 0)], [(1, 1)], [(0, 0), (0, 1)]
    )
    direct_a = lax.ppermute(send_a, "rep", swap1)
    direct_b = lax.ppermute(send_b, "rep", swap3)

    def relay(kept, relayed):
        return pl.pallas_call(
            relay_kernel,
            in_specs=[in_vmem] * 2,
            out_specs=in_vmem,
            out_shape=half_shape,
            compiler_params=params,
            name="relay",
        )(kept, relayed)

    second_a = lax.ppermute(relay(kept_a, relayed_a), "rep", swap3)
    second_b = lax.ppermute(relay(kept_b, relayed_b), "rep", swap1)
    presum = pl.pallas_call(
        presum_kernel,
        in_specs=[in_vmem] * 3,
        out_specs=in_vmem,
        out_shape=jax.ShapeDtypeStruct((per_row, rows, width), F32),
        compiler_params=params,
        name="presum",
    )(own, direct_a, direct_b)

    outgoing = pl.pallas_call(
        pack_kernel,
        in_specs=[pl.BlockSpec(memory_space=pl.ANY)] + [in_vmem] * 3,
        out_specs=in_vmem,
        out_shape=jax.ShapeDtypeStruct((fsdp * capacity, rows, width), BF16),
        scratch_shapes=[
            pltpu.VMEM((per_row, rows, width), BF16),
            pltpu.SMEM((per_row,), jnp.int32),
            pltpu.SemaphoreType.DMA,
        ],
        compiler_params=params,
        name="pack",
    )(slot_of, presum, second_a, second_b).reshape(fsdp, capacity, rows, width)

    arrived = lax.all_to_all(outgoing, "fsdp", split_axis=0, concat_axis=0, tiled=True)

    anywhere = pl.BlockSpec(memory_space=pl.ANY)
    factors = jax.ShapeDtypeStruct((capacity, order, order), F32)
    new_left, new_right, slot_update = pl.pallas_call(
        owner_kernel,
        in_specs=[in_vmem, in_vmem, in_vmem],
        out_specs=[anywhere, anywhere, in_vmem],
        out_shape=[factors, factors, jax.ShapeDtypeStruct((fsdp, capacity, rows, width), BF16)],
        scratch_shapes=[
            pltpu.VMEM((capacity, order, order), F32),
            pltpu.VMEM((capacity, order, order), F32),
            pltpu.SemaphoreType.DMA((2 * capacity,)),
        ],
        compiler_params=params,
        name="owner",
    )(arrived, left_factors[0, 0], right_factors[0, 0])

    returned = lax.all_to_all(slot_update, "fsdp", split_axis=0, concat_axis=0, tiled=True)

    mine_a, mine_b = pl.pallas_call(
        unpack_kernel,
        out_shape=[half_shape] * 2,
        grid_spec=pltpu.PrefetchScalarGridSpec(
            num_scalar_prefetch=1,
            grid=(1,),
            in_specs=[in_vmem],
            out_specs=[in_vmem, in_vmem],
        ),
        compiler_params=params,
        name="unpack",
    )(slot_of, returned.reshape(fsdp * capacity, rows, width))

    plus = [(i, (i + 1) % reps) for i in range(reps)]
    minus = [(i, (i - 1) % reps) for i in range(reps)]
    left_a = lax.ppermute(mine_a, "rep", plus)
    right_b = lax.ppermute(mine_b, "rep", minus)
    left_b = lax.ppermute(mine_b, "rep", plus)
    right_a = lax.ppermute(mine_a, "rep", minus)
    far_a = lax.ppermute(left_a, "rep", plus)
    far_b = lax.ppermute(right_b, "rep", minus)
    update_shape = jax.ShapeDtypeStruct((reps, 2, half, rows, width), BF16)

    def place(name, turns, halves, steps, values, before=None):
        held = [] if before is None else [before]
        size = len(steps[0])

        def where(i, t):
            turn, first = turns[-1], halves[-1]
            for k in range(len(steps) - 1):
                turn, first = jnp.where(i == k, turns[k], turn), jnp.where(i == k, halves[k], first)
            return lax.rem(t[0] + turn, reps), first, 0, 0, 0

        return pl.pallas_call(
            functools.partial(place_kernel, steps),
            out_shape=update_shape,
            grid_spec=pltpu.PrefetchScalarGridSpec(
                num_scalar_prefetch=1,
                grid=(len(steps),),
                in_specs=[in_vmem] * len(values) + [anywhere] * len(held),
                out_specs=pl.BlockSpec((1, size, half, rows, width), where),
            ),
            input_output_aliases={len(values) + 1: 0} if held else {},
            compiler_params=params,
            name=name,
        )(r[None], *values, *held)

    singles = [(0,), (1,), (2,), (3,)]
    update = place("place_first", [0, 0, 3, 1], [0, 1, 0, 1], singles, [mine_a, mine_b, left_a, right_b])
    update = place("place_second", [3, 1], [1, 0], singles[:2], [left_b, right_a], update)
    update = place("place_far", [2], [0], [(0, 1)], [far_a, far_b], update)
    return (update.reshape(reps * per_row, rows, width), new_left[None, None], new_right[None, None])


def solution(mesh):
    in_specs = (
        P("rep", None, "fsdp", None),
        P("rep", "fsdp", None, None, None),
        P("rep", "fsdp", None, None, None),
        P(),
    )
    out_specs = (
        P(None, "fsdp", None),
        P("rep", "fsdp", None, None, None),
        P("rep", "fsdp", None, None, None),
    )
    return jax.shard_map(shards, mesh=mesh, in_specs=in_specs, out_specs=out_specs, check_vma=False)
```

```python
import functools

import jax
import jax.numpy as jnp
from jax import lax
from jax.experimental import pallas as pl
from jax.experimental.pallas import tpu as pltpu
from jax.sharding import PartitionSpec as P

BF16 = jnp.bfloat16
F32 = jnp.float32
VMEM_BYTES = 36 * 1024 * 1024


def slots_of_blocks(owner_ids, capacity):
    position = jnp.arange(owner_ids.shape[0], dtype=jnp.int32)
    same_owner = owner_ids[:, None] == owner_ids[None, :]
    earlier = position[None, :] < position[:, None]
    slot_rank = jnp.sum((same_owner & earlier).astype(jnp.int32), axis=1)
    return owner_ids * capacity + slot_rank


def pick_kernel(places, table, parts, *refs):
    outs, sems = refs[:-1], refs[-1]
    copies = []
    for i, (k, h, target, row) in enumerate(places):
        copies.append(pltpu.make_async_copy(parts.at[table[0] ^ k, h], outs[target].at[row], sems.at[i]))
    for copy in copies:
        copy.start()
    for copy in copies:
        copy.wait()


def relay_kernel(kept, relayed, out):
    out[...] = (kept[0].astype(F32) + relayed[...].astype(F32)).astype(BF16)


def presum_kernel(own, direct_a, direct_b, out):
    half = direct_a.shape[1]
    for k, direct in enumerate((direct_a, direct_b)):
        out[k * half : (k + 1) * half] = own[k].astype(F32) + direct[0].astype(F32)


def pack_kernel(table, presum, second_a, second_b, out, held, slots, sem):
    half = second_a.shape[0]
    fetch = pltpu.make_async_copy(table, slots, sem)
    fetch.start()
    out[...] = jnp.zeros(out.shape, out.dtype)
    held[:half] = (presum[:half] + second_a[...].astype(F32)).astype(BF16)
    held[half:] = (presum[half:] + second_b[...].astype(F32)).astype(BF16)
    fetch.wait()

    def move(j, carry):
        out[slots[j]] = held[j]
        return carry

    lax.fori_loop(0, 2 * half, move, 0, unroll=8)


def dot(a, b, ca=1, cb=0):
    return lax.dot_general(a, b, (((ca,), (cb,)), ((), ())), preferred_element_type=F32)


def inverse_roots(matrices, identity):
    scales = [lax.rsqrt(jnp.sum(m * m) + 1e-06) for m in matrices]
    ybs = [(m * c).astype(BF16) for m, c in zip(matrices, scales)]
    y2s = [dot(b, b) for b in ybs]
    ss = [
        (2.25 * c) * m - 1.5 * y2 + 0.25 * dot(y2.astype(BF16), b)
        for m, c, y2, b in zip(matrices, scales, y2s, ybs)
    ]
    sbs = [s.astype(BF16) for s in ss]
    s2s = [dot(s, s) for s in sbs]
    qs = [
        -2.4375 * s + 1.6875 * s2 + dot((0.0625 * s2 - 0.5625 * s).astype(BF16), s2.astype(BF16))
        for s, s2 in zip(ss, s2s)
    ]
    zs = [
        3.375 * identity + 1.5 * q - (1.125 * c) * m - 0.5 * dot(q.astype(BF16), b)
        for q, m, c, b in zip(qs, matrices, scales, ybs)
    ]
    return [z.astype(BF16) for z in zs]


def owner_kernel(arrived, left, right, new_left, new_right, out, held_left, held_right, sems):
    capacity, n = left.shape[0], left.shape[1]
    row = lax.broadcasted_iota(jnp.int32, (n, n), 0)
    col = lax.broadcasted_iota(jnp.int32, (n, n), 1)
    identity = (row == col).astype(F32)
    wides = [arrived[:, s].astype(F32).reshape(n, n) for s in range(capacity)]
    grads = [wide.astype(BF16) for wide in wides]
    norms = [jnp.sum(wide * wide) for wide in wides]
    turned = [grad.T for grad in grads]
    grams = [dot(g, g, 1, 1) for pair in zip(grads, turned) for g in pair]
    factors = [0.9 * (left, right)[k % 2][k // 2] + 0.1 * gram for k, gram in enumerate(grams)]
    copies = []
    for k, factor in enumerate(factors):
        held, target = ((held_left, new_left), (held_right, new_right))[k % 2]
        held[k // 2] = factor
        copies.append(pltpu.make_async_copy(held.at[k // 2], target.at[k // 2], sems.at[k]))
        copies[-1].start()
    roots = inverse_roots(factors, identity)
    halves = [dot(root_left, grad).astype(BF16) for root_left, grad in zip(roots[::2], grads)]
    raws = [dot(half, root_right) for half, root_right in zip(halves, roots[1::2])]
    for s, raw in enumerate(raws):
        scale = jnp.sqrt(norms[s]) * lax.rsqrt(jnp.sum(raw * raw) + 1e-06)
        out[:, s] = (raw * scale).reshape(out.shape[0], out.shape[2], out.shape[3]).astype(BF16)
    for copy in copies:
        copy.wait()


def unpack_kernel(table, rows, out_a, out_b, slots, sem):
    half = out_a.shape[0]
    fetch = pltpu.make_async_copy(table, slots, sem)
    fetch.start()
    fetch.wait()

    def move(j, carry):
        out_a[j] = rows[slots[j]]
        out_b[j] = rows[slots[half + j]]
        return carry

    lax.fori_loop(0, half, move, 0, unroll=8)


def place_kernel(steps, table, *refs):
    out = refs[-1]
    for k, step in enumerate(steps):

        @pl.when(pl.program_id(0) == k)
        def _():
            for i, part in enumerate(step):
                out[0, i] = refs[part][...]


def shards(grads, left_factors, right_factors, owners):
    reps = lax.axis_size("rep")
    fsdp = lax.axis_size("fsdp")
    r = lax.axis_index("rep").astype(jnp.int32)
    rows, width = grads.shape[2], grads.shape[3]
    capacity, order = left_factors.shape[2], left_factors.shape[3]
    per_row = grads.shape[1] // reps
    half = per_row // 2
    own_owners = lax.dynamic_index_in_dim(owners[:, :, 0], r, 0, keepdims=False)
    slot_of = slots_of_blocks(own_owners, capacity)

    swap1 = [(i, i ^ 1) for i in range(reps)]
    swap3 = [(i, i ^ 3) for i in range(reps)]
    parts = grads.reshape(reps, 2, half, rows, width)
    params = pltpu.CompilerParams(vmem_limit_bytes=VMEM_BYTES)
    half_shape = jax.ShapeDtypeStruct((half, rows, width), BF16)

    in_vmem = pl.BlockSpec(memory_space=pltpu.VMEM)
    in_hbm = pl.BlockSpec(memory_space=pltpu.HBM)

    def pick(name, *groups):
        places = [(k, h, o, i) for o, group in enumerate(groups) for i, (k, h) in enumerate(group)]
        return pl.pallas_call(
            functools.partial(pick_kernel, places),
            out_shape=[jax.ShapeDtypeStruct((len(group), half, rows, width), BF16) for group in groups],
            grid_spec=pltpu.PrefetchScalarGridSpec(
                num_scalar_prefetch=1,
                grid=(1,),
                in_specs=[in_hbm],
                out_specs=[in_vmem] * len(groups),
                scratch_shapes=[pltpu.SemaphoreType.DMA((len(places),))],
            ),
            compiler_params=params,
            name=name,
        )(r[None], parts)

    def opposite(h):
        return lax.dynamic_slice(parts, (r ^ 2, h, 0, 0, 0), (1, 1, half, rows, width))[0, 0]

    relayed_a = lax.ppermute(opposite(0), "rep", swap1)
    relayed_b = lax.ppermute(opposite(1), "rep", swap3)
    send_a, send_b, kept_a, kept_b, own = pick(
        "pick", [(1, 0)], [(3, 1)], [(3, 0)], [(1, 1)], [(0, 0), (0, 1)]
    )
    direct_a = lax.ppermute(send_a, "rep", swap1)
    direct_b = lax.ppermute(send_b, "rep", swap3)

    def relay(kept, relayed):
        return pl.pallas_call(
            relay_kernel,
            in_specs=[in_vmem] * 2,
            out_specs=in_vmem,
            out_shape=half_shape,
            compiler_params=params,
            name="relay",
        )(kept, relayed)

    second_a = lax.ppermute(relay(kept_a, relayed_a), "rep", swap3)
    second_b = lax.ppermute(relay(kept_b, relayed_b), "rep", swap1)
    presum = pl.pallas_call(
        presum_kernel,
        in_specs=[in_vmem] * 3,
        out_specs=in_vmem,
        out_shape=jax.ShapeDtypeStruct((per_row, rows, width), F32),
        compiler_params=params,
        name="presum",
    )(own, direct_a, direct_b)

    outgoing = pl.pallas_call(
        pack_kernel,
        in_specs=[pl.BlockSpec(memory_space=pl.ANY)] + [in_vmem] * 3,
        out_specs=in_vmem,
        out_shape=jax.ShapeDtypeStruct((fsdp * capacity, rows, width), BF16),
        scratch_shapes=[
            pltpu.VMEM((per_row, rows, width), BF16),
            pltpu.SMEM((per_row,), jnp.int32),
            pltpu.SemaphoreType.DMA,
        ],
        compiler_params=params,
        name="pack",
    )(slot_of, presum, second_a, second_b).reshape(fsdp, capacity, rows, width)

    arrived = lax.all_to_all(outgoing, "fsdp", split_axis=0, concat_axis=0, tiled=True)

    anywhere = pl.BlockSpec(memory_space=pl.ANY)
    factors = jax.ShapeDtypeStruct((capacity, order, order), F32)
    new_left, new_right, slot_update = pl.pallas_call(
        owner_kernel,
        in_specs=[in_vmem, in_vmem, in_vmem],
        out_specs=[anywhere, anywhere, in_vmem],
        out_shape=[factors, factors, jax.ShapeDtypeStruct((fsdp, capacity, rows, width), BF16)],
        scratch_shapes=[
            pltpu.VMEM((capacity, order, order), F32),
            pltpu.VMEM((capacity, order, order), F32),
            pltpu.SemaphoreType.DMA((2 * capacity,)),
        ],
        compiler_params=params,
        name="owner",
    )(arrived, left_factors[0, 0], right_factors[0, 0])

    returned = lax.all_to_all(slot_update, "fsdp", split_axis=0, concat_axis=0, tiled=True)

    mine_a, mine_b = pl.pallas_call(
        unpack_kernel,
        in_specs=[anywhere, in_vmem],
        out_specs=[in_vmem, in_vmem],
        out_shape=[half_shape] * 2,
        scratch_shapes=[pltpu.SMEM((per_row,), jnp.int32), pltpu.SemaphoreType.DMA],
        compiler_params=params,
        name="unpack",
    )(slot_of, returned.reshape(fsdp * capacity, rows, width))

    plus = [(i, (i + 1) % reps) for i in range(reps)]
    minus = [(i, (i - 1) % reps) for i in range(reps)]
    left_a = lax.ppermute(mine_a, "rep", plus)
    right_b = lax.ppermute(mine_b, "rep", minus)
    left_b = lax.ppermute(mine_b, "rep", plus)
    right_a = lax.ppermute(mine_a, "rep", minus)
    far_a = lax.ppermute(left_a, "rep", plus)
    far_b = lax.ppermute(right_b, "rep", minus)
    update_shape = jax.ShapeDtypeStruct((reps, 2, half, rows, width), BF16)

    def place(name, turns, halves, steps, values, before=None):
        held = [] if before is None else [before]
        size = len(steps[0])

        def where(i, t):
            turn, first = turns[-1], halves[-1]
            for k in range(len(steps) - 1):
                turn, first = jnp.where(i == k, turns[k], turn), jnp.where(i == k, halves[k], first)
            return lax.rem(t[0] + turn, reps), first, 0, 0, 0

        return pl.pallas_call(
            functools.partial(place_kernel, steps),
            out_shape=update_shape,
            grid_spec=pltpu.PrefetchScalarGridSpec(
                num_scalar_prefetch=1,
                grid=(len(steps),),
                in_specs=[in_vmem] * len(values) + [anywhere] * len(held),
                out_specs=pl.BlockSpec((1, size, half, rows, width), where),
            ),
            input_output_aliases={len(values) + 1: 0} if held else {},
            compiler_params=params,
            name=name,
        )(r[None], *values, *held)

    singles = [(0,), (1,), (2,), (3,)]
    update = place("place_first", [0, 0, 3, 1], [0, 1, 0, 1], singles, [mine_a, mine_b, left_a, right_b])
    update = place("place_second", [3, 1], [1, 0], singles[:2], [left_b, right_a], update)
    update = place("place_far", [2], [0], [(0, 1)], [far_a, far_b], update)
    return (update.reshape(reps * per_row, rows, width), new_left[None, None], new_right[None, None])


def solution(mesh):
    in_specs = (
        P("rep", None, "fsdp", None),
        P("rep", "fsdp", None, None, None),
        P("rep", "fsdp", None, None, None),
        P(),
    )
    out_specs = (
        P(None, "fsdp", None),
        P("rep", "fsdp", None, None, None),
        P("rep", "fsdp", None, None, None),
    )
    return jax.shard_map(shards, mesh=mesh, in_specs=in_specs, out_specs=out_specs, check_vma=False)
```
